32 devices in a mesh: dp: 16 (over z, x, core), blk: 2 (over y).
Axes of the slice: x: 2, y: 2, z: 4, core: 2. Of those that a mesh axis runs over, the one named last changes fastest.
Arguments:
- segment: bfloat16 [16, 960, 1024], P('dp', 'blk'), may hold values from -6 to 6
- memory: bfloat16 [16, 960, 1024], P('dp', 'blk'), may hold values from -6 to 6
- comp_memory: bfloat16 [16, 512, 1024], P('dp', 'blk'), may hold values from -6 to 6
- mem_start: int32 [16], P('dp'), may hold values from 0 to 512
- first_gain: bfloat16 [1024], replicated, may hold values from 0.5 to 1.5
- first_bias: bfloat16 [1024], replicated, may hold values from -1.25 to 1.25
- w_query: bfloat16 [1024, 1024], replicated, may hold values from -0.1875 to 0.1875
- w_key: bfloat16 [1024, 1024], replicated, may hold values from -0.1875 to 0.1875
- w_value: bfloat16 [1024, 1024], replicated, may hold values from -0.1875 to 0.1875
- w_rel: bfloat16 [1024, 1024], replicated, may hold values from -0.1875 to 0.1875
- u_bias: bfloat16 [1024], replicated, may hold values from -3 to 3
- v_bias: bfloat16 [1024], replicated, may hold values from -3 to 3
- w_out: bfloat16 [1024, 1024], replicated, may hold values from -1.5 to 1.5
- second_gain: bfloat16 [1024], replicated, may hold values from 0.5 to 1.5
- second_bias: bfloat16 [1024], replicated, may hold values from -1.25 to 1.25
- w_up: bfloat16 [1024, 4096], replicated, may hold values from -0.1875 to 0.1875
- b_up: bfloat16 [4096], replicated, may hold values from -1.25 to 1.25
- w_down: bfloat16 [4096, 1024], replicated, may hold values from -0.09375 to 0.09375
- b_down: bfloat16 [1024], replicated, may hold values from -1.75 to 1.75
- w_comp: bfloat16 [3072, 1024], replicated, may hold values from -0.109375 to 0.109375
- b_comp: bfloat16 [1024], replicated, may hold values from -1.75 to 1.75
- cot_out: bfloat16 [16, 960, 1024], P('dp', 'blk'), may hold values from -6 to 6
- cot_comp: bfloat16 [16, 320, 1024], P('dp', 'blk'), may hold values from -6 to 6
Outputs:
- layer_out: bfloat16 [16, 960, 1024], P('dp', 'blk')
- d_segment: bfloat16 [16, 960, 1024], P('dp', 'blk')
- new_compressed: bfloat16 [16, 320, 1024], P('dp', 'blk')
- grad_first_gain: float32 [1024], replicated
- grad_first_bias: float32 [1024], replicated
- grad_w_query: float32 [1024, 1024], replicated
- grad_w_key: float32 [1024, 1024], replicated
- grad_w_value: float32 [1024, 1024], replicated
- grad_w_rel: float32 [1024, 1024], replicated
- grad_u_bias: float32 [1024], replicated
- grad_v_bias: float32 [1024], replicated
- grad_w_out: float32 [1024, 1024], replicated
- grad_second_gain: float32 [1024], replicated
- grad_second_bias: float32 [1024], replicated
- grad_w_up: float32 [1024, 4096], replicated
- grad_b_up: float32 [4096], replicated
- grad_w_down: float32 [4096, 1024], replicated
- grad_b_down: float32 [1024], replicated
- grad_w_comp: float32 [3072, 1024], replicated
- grad_b_comp: float32 [1024], replicated
The draws below stay inside these ranges and needn't reach their ends.
All inputs are finite; a program needn't handle non-finite values.
Results may differ from the reference program's by a relative error of at most 0.017.
Values may be sent and summed in bfloat16 or wider, within the bound.
No kernel may reach another device: no remote copies, remote signals or barrier semaphores. Data moves between devices by JAX's collectives and lax.ppermute only.
A program may use at most 448 MiB of HBM per device.

```python
from functools import partial
import jax
import jax.numpy as jnp
from jax import lax

D = 1024
H = 8
DH = 128
FF = 4096
SEG = 960
MEM = 960
CMEM = 512
RATE = 3
KEYS = 2432
NREL = 3391
CNEW = 320
STREAMS = 16


def set_ends(drawn, key, smallest, largest):
    place = [jax.random.randint(jax.random.fold_in(key, axis), (), 0, length) for axis, length in enumerate(drawn.shape)]
    widest = drawn.shape.index(max(drawn.shape))
    neighbour = place[:widest] + [(place[widest] + 1) % drawn.shape[widest]] + place[widest + 1:]
    return drawn.at[tuple(place)].set(smallest).at[tuple(neighbour)].set(largest)


def spiked(values, key, source, target, parts, factor):
    def block_of(dim):
        return (jnp.arange(values.shape[dim]) // (values.shape[dim] // parts)).reshape((-1,) + (1,) * (values.ndim - 1 - dim))

    near = jax.random.permutation(key, parts)[block_of(target)]
    other_side = (block_of(target) + parts // 2) % parts
    return jnp.where((block_of(source) == near) | (block_of(source) == other_side), factor * values, values)


def steps_of(stream_key, shape, pieces, low, largest):
    level, own = 1.0, jax.random.fold_in(stream_key, 6)
    for axis_at, parts in pieces:
        steps = jnp.exp(jax.random.uniform(jax.random.fold_in(own, axis_at), (parts,), jnp.float32, low / len(pieces), largest / len(pieces)))
        level = level * jnp.repeat(steps, shape[axis_at] // parts).reshape([-1 if axis == axis_at else 1 for axis in range(len(shape))])
    return level


def scatter_about(rng, dims, width, reach, cuts=(), kind=jnp.bfloat16):
    array = jax.random.normal(rng, dims, jnp.float32) * width
    if len(cuts) > 0:
        array = steps_of(rng, dims, cuts, -0.22, 0.18) * array
    return jnp.clip(array, min=-reach, max=reach).astype(kind)


def bell_draw_with(own_key, extent, spread, bound, split, heavy, kind=jnp.bfloat16):
    array = spread * jax.random.normal(own_key, extent, jnp.float32)
    if split:
        array = array * steps_of(own_key, extent, split, -0.22, 0.18)
    return jnp.clip(spiked(array, jax.random.fold_in(own_key, 3), *heavy), -bound, bound).astype(kind)


def setup_inputs(seed: int = 0) -> dict:
    key_of = jax.random.split(jax.random.key(seed), 24)
    return {
        "segment": bell_draw_with(key_of[0], (STREAMS, SEG, D), 1.0, 6.0, ((0, 16), (1, 2)), (0, 2, 16, 2.0)),
        "memory": scatter_about(key_of[1], (STREAMS, MEM, D), 1.0, 6.0, ((0, 16), (1, 2))),
        "comp_memory": scatter_about(key_of[2], (STREAMS, CMEM, D), 1.0, 6.0, ((0, 16), (1, 2))),
        "mem_start": set_ends(jax.random.randint(key_of[3], (STREAMS,), 0, CMEM + 1), jax.random.fold_in(key_of[3], 1), 0, CMEM).astype(jnp.int32),
        "first_gain": jnp.clip(1.0 + 0.1 * jax.random.normal(key_of[4], (D,), jnp.float32), 0.5, 1.5).astype(jnp.bfloat16),
        "first_bias": scatter_about(key_of[5], (D,), 0.2, 1.25),
        "w_query": scatter_about(key_of[6], (D, D), D ** -0.5, 0.1875),
        "w_key": scatter_about(key_of[7], (D, D), D ** -0.5, 0.1875),
        "w_value": scatter_about(key_of[8], (D, D), D ** -0.5, 0.1875),
        "w_rel": scatter_about(key_of[9], (D, D), D ** -0.5, 0.1875),
        "u_bias": scatter_about(key_of[10], (D,), 0.5, 3.0),
        "v_bias": scatter_about(key_of[11], (D,), 0.5, 3.0),
        "w_out": scatter_about(key_of[12], (D, D), (D // 64) ** -0.5, 1.5),
        "second_gain": jnp.clip(1.0 + 0.1 * jax.random.normal(key_of[13], (D,), jnp.float32), 0.5, 1.5).astype(jnp.bfloat16),
        "second_bias": scatter_about(key_of[14], (D,), 0.2, 1.25),
        "w_up": scatter_about(key_of[15], (D, FF), D ** -0.5, 0.1875),
        "b_up": scatter_about(key_of[16], (FF,), 0.2, 1.25),
        "w_down": scatter_about(key_of[17], (FF, D), FF ** -0.5, 0.09375),
        "b_down": scatter_about(key_of[18], (D,), 0.3, 1.75),
        "w_comp": scatter_about(key_of[19], (RATE * D, D), (RATE * D) ** -0.5, 0.109375),
        "b_comp": scatter_about(key_of[20], (D,), 0.3, 1.75),
        "cot_out": bell_draw_with(key_of[21], (STREAMS, SEG, D), 1.0, 6.0, ((0, 16), (1, 2)), (0, 2, 16, 2.0)),
        "cot_comp": scatter_about(key_of[22], (STREAMS, CNEW, D), 1.0, 6.0, ((0, 16), (1, 2))),
    }


@jax.custom_vjp
def low(v):
    return lax.optimization_barrier(v.astype(jnp.bfloat16)).astype(jnp.float32)

@jax.custom_vjp
def low_back(v):
    return v

def low_keep(v):
    return (low(v), None)

def low_pass(kept, grad):
    return (grad,)

def back_keep(v):
    return (v, None)

def back_low(kept, grad):
    return (low(grad),)
low.defvjp(low_keep, low_pass)
low_back.defvjp(back_keep, back_low)

def matmul(left, right):
    return jnp.dot(left, right, precision=lax.Precision.HIGHEST, preferred_element_type=jnp.float32)

def layer_norm(values, gain, bias):
    centred = values - lax.optimization_barrier(jnp.mean(values, -1, keepdims=True))
    return centred * lax.rsqrt(lax.optimization_barrier(jnp.mean(centred * centred, -1, keepdims=True)) + 1e-05) * gain + bias

def sinus_table():
    offsets = jnp.arange(NREL, dtype=jnp.float32)
    distance = KEYS - 1 - offsets
    frequency = 10000.0 ** (-2.0 * jnp.arange(D // 2, dtype=jnp.float32) / D)
    angles = distance[:, None] * frequency[None, :]
    wave_table = jnp.concatenate([jnp.sin(angles), jnp.cos(angles)], -1)
    return lax.optimization_barrier(wave_table.astype(jnp.bfloat16)).astype(jnp.float32)

def skew(table_scores, row_count, col_count):
    leading = table_scores.shape[:-2]
    padded = jnp.pad(table_scores, [(0, 0)] * len(leading) + [(0, 0), (0, 1)])
    flattened = padded.reshape(leading + (row_count * (row_count + col_count),))
    flattened = flattened[..., row_count - 1:row_count - 1 + row_count * (row_count + col_count - 1)]
    return flattened.reshape(leading + (row_count, row_count + col_count - 1))[..., :col_count]

def stream_layer(weights, relative, stream):
    first_gain, first_bias, w_query, w_key, w_value, u_bias, v_bias, w_out, second_gain, second_bias, w_up, b_up, w_down, b_down = weights
    segment, memory, comp_memory, mem_start = stream
    keys_in = jnp.concatenate([comp_memory, memory, segment], 0)
    normed = low(layer_norm(keys_in, first_gain, first_bias))
    query_rows = low_back(matmul(normed[CMEM + MEM:], w_query))
    q_content = low(query_rows + u_bias).reshape(SEG, H, DH)
    q_position = low(query_rows + v_bias).reshape(SEG, H, DH)
    key_heads = low_back(low(matmul(normed, w_key))).reshape(KEYS, H, DH)
    value_heads = low_back(low(matmul(normed, w_value))).reshape(KEYS, H, DH)
    content = jnp.einsum('qhd,khd->hqk', q_content, key_heads, precision=lax.Precision.HIGHEST)
    table_scores = jnp.einsum('qhd,whd->hqw', q_position, relative, precision=lax.Precision.HIGHEST)
    position = skew(table_scores, SEG, KEYS)
    scores = low_back((content + position) * DH ** (-0.5))
    key_place = jnp.arange(KEYS)
    query_place = CMEM + MEM + jnp.arange(SEG)
    allowed = (key_place[None, :] >= mem_start) & (key_place[None, :] <= query_place[:, None])
    attention = jax.nn.softmax(jnp.where(allowed[None], scores, -1e+30), axis=-1)
    attended = jnp.einsum('hqk,khd->qhd', low(attention), value_heads, precision=lax.Precision.HIGHEST)
    attended = low_back(low(attended.reshape(SEG, D)))
    branch = low_back(matmul(attended, w_out))
    hidden = segment + branch
    second_normed = low(layer_norm(hidden, second_gain, second_bias))
    pre_gelu = low_back(matmul(second_normed, w_up) + b_up)
    gelu_out = low(jax.nn.gelu(pre_gelu, approximate=True))
    return hidden + matmul(gelu_out, w_down) + b_down

def reference(segment, memory, comp_memory, mem_start, first_gain, first_bias, w_query, w_key, w_value, w_rel, u_bias, v_bias, w_out, second_gain, second_bias, w_up, b_up, w_down, b_down, w_comp, b_comp, cot_out, cot_comp):
    params = tuple((param.astype(jnp.float32) for param in (first_gain, first_bias, w_query, w_key, w_value, w_rel, u_bias, v_bias, w_out, second_gain, second_bias, w_up, b_up, w_down, b_down, w_comp, b_comp)))
    memory_wide = memory.astype(jnp.float32)
    comp_wide = comp_memory.astype(jnp.float32)
    sinus = sinus_table()

    def forward(weights, segment_wide):
        relative = low(matmul(sinus, weights[5])).reshape(NREL, H, DH)
        layer_weights = weights[:5] + weights[6:15]
        per_stream = jax.checkpoint(partial(stream_layer, layer_weights, relative))
        output = lax.map(per_stream, (segment_wide, memory_wide, comp_wide, mem_start))
        windows = memory_wide.reshape(STREAMS, MEM // RATE, RATE * D)
        compressed = jnp.einsum('snk,kd->snd', windows, weights[15], precision=lax.Precision.HIGHEST) + weights[16]
        return (output, compressed)
    (output, compressed), pullback = jax.vjp(forward, params, segment.astype(jnp.float32))
    grads, d_segment = pullback((cot_out.astype(jnp.float32), cot_comp.astype(jnp.float32)))
    return (output.astype(jnp.bfloat16), d_segment.astype(jnp.bfloat16), compressed.astype(jnp.bfloat16), grads[0], grads[1], grads[2], grads[3], grads[4], grads[5], grads[6], grads[7], grads[8], grads[9], grads[10], grads[11], grads[12], grads[13], grads[14], grads[15], grads[16])
```

```python
from functools import partial

import jax
import jax.numpy as jnp
from jax import lax
from jax.experimental import pallas as pl
from jax.experimental.pallas import tpu as pltpu
from jax.sharding import PartitionSpec as P

D = 1024
H = 8
DH = 128
MEM = 960
CMEM = 512
RATE = 3
KEYS = 2432

TILE = 192
epsilon = 1e-05
negative = -1e30
wide = jnp.float32
narrow = jnp.bfloat16


def tiles_of(seg, keys, tile):
    tiles = []
    for first in range(0, seg, tile):
        used = keys - seg + first + tile
        cols = -(-used // 128) * 128
        tiles.append((first, cols, keys - cols, cols - used))
    return tiles


def dot(left, right, left_dim, right_dim):
    return lax.dot_general(
        left, right, (((left_dim,), (right_dim,)), ((), ())), preferred_element_type=wide
    )


def unskew(grid, tile, cols, pad):
    parts = []
    for group in range(tile // 8):
        shift = tile - 1 + pad - 8 * group - 7
        rows = grid[8 * group : 8 * group + 8]
        parts.append(pltpu.roll(rows, shift, 1) if shift else rows)
    moved = jnp.concatenate(parts, 0)
    left = 7 - (lax.broadcasted_iota(jnp.int32, (tile, cols), 0) & 7)
    for bit in range(3):
        moved = jnp.where((left & (1 << bit)) != 0, pltpu.roll(moved, 1 << bit, 1), moved)
    return moved


def attend_kernel(seg, keys, start_ref, qc_ref, qp_ref, kv_ref, rel_ref, out_ref, probs_ref):
    past = keys - seg
    factor = DH**-0.5 * 1.4426950408889634
    start = start_ref[0]
    for first, cols, base, pad in tiles_of(seg, keys, TILE):
        rows = pl.ds(first, TILE)
        content = dot(qc_ref[rows, :], kv_ref[0:cols, 0:DH], 1, 1)
        table = dot(qp_ref[rows, :], rel_ref[base : base + cols, :], 1, 1)
        table = pltpu.roll(table, cols - (TILE - 1 + pad), 1, stride=1, stride_axis=0)
        scores = content + table
        left = scores[:, :CMEM]
        lane = lax.broadcasted_iota(jnp.int32, left.shape, 1)
        left = jnp.where(lane >= start, left, negative)
        edge = (past + first) // 128 * 128
        right = scores[:, edge:]
        lane = lax.broadcasted_iota(jnp.int32, right.shape, 1) + (edge - past - first)
        row = lax.broadcasted_iota(jnp.int32, right.shape, 0)
        right = jnp.where(lane <= row, right, negative)
        scores = jnp.concatenate([left, scores[:, CMEM:edge], right], 1)
        largest = jnp.max(scores, -1, keepdims=True)
        probs = jnp.exp2(scores * factor - largest * factor)
        probs = (probs * (1.0 / jnp.sum(probs, -1, keepdims=True))).astype(narrow)
        probs_ref[0, rows, 0:cols] = probs
        out_ref[rows, :] = dot(probs, kv_ref[0:cols, DH:], 1, 0).astype(narrow)


def attend(start, q_content, q_position, key_value, relative):
    seg, width = q_content.shape
    keys, heads = key_value.shape[0], width // DH
    per_query = pl.BlockSpec((seg, DH), lambda h: (0, h))
    flops = 6 * heads * seg * keys * DH
    return pl.pallas_call(
        partial(attend_kernel, seg, keys),
        grid=(heads,),
        in_specs=[
            pl.BlockSpec(memory_space=pltpu.SMEM),
            per_query,
            per_query,
            pl.BlockSpec((keys, 2 * DH), lambda h: (0, h)),
            pl.BlockSpec((keys, DH), lambda h: (0, h)),
        ],
        out_specs=[per_query, pl.BlockSpec((1, seg, keys), lambda h: (h, 0, 0))],
        out_shape=[
            jax.ShapeDtypeStruct((seg, width), narrow),
            jax.ShapeDtypeStruct((heads, seg, keys), narrow),
        ],
        compiler_params=pltpu.CompilerParams(vmem_limit_bytes=56 << 20),
        cost_estimate=pl.CostEstimate(
            flops=flops, bytes_accessed=32 << 20, transcendentals=heads * seg * keys
        ),
        name="attend",
    )(start, q_content, q_position, key_value, relative)


def attend_back_kernel(
    seg,
    keys,
    probs_ref,
    qc_ref,
    qp_ref,
    kv_ref,
    rel_ref,
    da_ref,
    dq_ref,
    dkv_ref,
    drel_ref,
    gu_ref,
    gv_ref,
    key_sum,
    value_sum,
    rel_sum,
):
    scale = DH**-0.5
    grad_u = jnp.zeros((1, DH), wide)
    grad_v = jnp.zeros((1, DH), wide)
    for step, (first, cols, base, pad) in enumerate(tiles_of(seg, keys, TILE)[::-1]):
        rows = pl.ds(first, TILE)
        probs = probs_ref[0, rows, 0:cols]
        probs_wide = probs.astype(wide)
        d_out, qc, qp = da_ref[rows, :], qc_ref[rows, :], qp_ref[rows, :]
        d_probs = dot(d_out, kv_ref[0:cols, DH:], 1, 1)
        weighted = probs_wide * d_probs
        d_scores = weighted - probs_wide * jnp.sum(weighted, -1, keepdims=True)
        d_low = d_scores.astype(narrow)
        d_table = unskew(d_scores, TILE, cols, pad).astype(narrow)
        d_content = dot(d_low, kv_ref[0:cols, 0:DH], 1, 0)
        d_position = dot(d_table, rel_ref[base : base + cols, :], 1, 0)
        grad_u += jnp.sum(d_content, 0, keepdims=True)
        grad_v += jnp.sum(d_position, 0, keepdims=True)
        dq_ref[rows, :] = ((d_content + d_position) * scale).astype(narrow)
        d_key = dot(qc, d_low, 0, 0)
        d_value = dot(d_out, probs, 0, 0)
        d_rel = dot(qp, d_table, 0, 0)
        if step == 0:
            key_sum[...] = d_key
            value_sum[...] = d_value
            rel_sum[...] = d_rel
        else:
            key_sum[:, 0:cols] += d_key
            value_sum[:, 0:cols] += d_value
            rel_sum[:, base : base + cols] += d_rel
    dkv_ref[:, 0:DH] = (key_sum[...] * scale).T.astype(narrow)
    dkv_ref[:, DH:] = value_sum[...].T.astype(narrow)
    drel_ref[...] = (rel_sum[...] * scale).T.astype(narrow)
    gu_ref[...] = grad_u * scale
    gv_ref[...] = grad_v * scale


def attend_back(probs, q_content, q_position, key_value, relative, d_attended):
    seg, width = q_content.shape
    keys, heads = key_value.shape[0], width // DH
    per_query = pl.BlockSpec((seg, DH), lambda h: (0, h))
    per_pair = pl.BlockSpec((keys, 2 * DH), lambda h: (0, h))
    per_key = pl.BlockSpec((keys, DH), lambda h: (0, h))
    per_head = pl.BlockSpec((1, DH), lambda h: (0, h))
    return pl.pallas_call(
        partial(attend_back_kernel, seg, keys),
        grid=(heads,),
        in_specs=[
            pl.BlockSpec((1, seg, keys), lambda h: (h, 0, 0)),
            per_query,
            per_query,
            per_pair,
            per_key,
            per_query,
        ],
        out_specs=[per_query, per_pair, per_key, per_head, per_head],
        out_shape=[
            jax.ShapeDtypeStruct((seg, width), narrow),
            jax.ShapeDtypeStruct((keys, 2 * width), narrow),
            jax.ShapeDtypeStruct((keys, width), narrow),
            jax.ShapeDtypeStruct((1, width), wide),
            jax.ShapeDtypeStruct((1, width), wide),
        ],
        scratch_shapes=[pltpu.VMEM((DH, keys), wide)] * 3,
        compiler_params=pltpu.CompilerParams(vmem_limit_bytes=60 << 20),
        cost_estimate=pl.CostEstimate(
            flops=12 * heads * seg * keys * DH, bytes_accessed=40 << 20, transcendentals=0
        ),
        name="attend_back",
    )(probs, q_content, q_position, key_value, relative, d_attended)


def swap(value, axis, bit=0):
    pairs = [(source, source ^ (1 << bit)) for source in range(lax.axis_size(axis))]
    return lax.ppermute(value, axis, pairs)


def side(axis, bit=0):
    return (lax.axis_index(axis) >> bit) & 1


def axis_bits():
    count = lax.axis_size("dp").bit_length() - 1
    core = [("dp", 0)]
    near = [("dp", bit) for bit in range(1, min(2, count))]
    rest = [("dp", bit) for bit in range(2, count)]
    return core, near, [("blk", 0)], rest


def scatter_sum(value, steps):
    for axis, bit in steps:
        half = value.shape[0] // 2
        which = side(axis, bit)
        theirs = lax.dynamic_slice_in_dim(value, (1 - which) * half, half, 0)
        ours = lax.dynamic_slice_in_dim(value, which * half, half, 0)
        value = (ours.astype(wide) + swap(theirs, axis, bit).astype(wide)).astype(narrow)
    return value


def in_order(which, ours, theirs, dim=0):
    return jnp.where(
        which == 0,
        jnp.concatenate([ours, theirs], dim),
        jnp.concatenate([theirs, ours], dim),
    )


def gather_back(value, steps):
    for axis, bit in reversed(steps):
        value = in_order(side(axis, bit), value, swap(value, axis, bit))
    return value


def sum_over_all(value):
    core, near, blk, rest = axis_bits()
    for axis, bit in core + near + blk + rest:
        value = value + swap(value, axis, bit)
    return value


def moments(values):
    centred = values - jnp.mean(values, -1, keepdims=True)
    inverse = lax.rsqrt(jnp.mean(centred * centred, -1, keepdims=True) + epsilon)
    return centred * inverse, inverse


def norm_back(grad, normal, inverse, gain):
    scaled = grad * gain
    inner = (
        scaled
        - jnp.mean(scaled, -1, keepdims=True)
        - normal * jnp.mean(scaled * normal, -1, keepdims=True)
    )
    return inner * inverse


def sinus_table():
    fine = 64
    frequency = 10000.0 ** (-2.0 * jnp.arange(D // 2, dtype=wide) / D)
    coarse_place = KEYS - 1 - fine * jnp.arange(KEYS // fine, dtype=wide)
    fine_place = jnp.arange(fine, dtype=wide)
    coarse = (coarse_place[:, None] * frequency[None, :])[:, None, :]
    little = (fine_place[:, None] * frequency[None, :])[None, :, :]
    sin_a, cos_a, sin_b, cos_b = lax.optimization_barrier(
        (jnp.sin(coarse), jnp.cos(coarse), jnp.sin(little), jnp.cos(little))
    )
    sine = sin_a * cos_b - cos_a * sin_b
    cosine = cos_a * cos_b + sin_a * sin_b
    return jnp.concatenate([sine, cosine], -1).astype(narrow).reshape(KEYS, D)


def matmul(left, right):
    return jnp.dot(left, right, preferred_element_type=wide)


def outer(left, right):
    return dot(left, right, 0, 0)


def back_through(grad, weight):
    return dot(grad, weight, 1, 1)


def on_device(
    segment,
    memory,
    comp_memory,
    mem_start,
    first_gain,
    first_bias,
    w_query,
    w_key,
    w_value,
    w_rel,
    u_bias,
    v_bias,
    w_out,
    second_gain,
    second_bias,
    w_up,
    b_up,
    w_down,
    b_down,
    w_comp,
    b_comp,
    cot_out,
    cot_comp,
):
    here = lax.axis_index("blk")
    blocks = lax.axis_size("blk")
    segment, memory, comp_memory = segment[0], memory[0], comp_memory[0]
    cot_out, cot_comp = cot_out[0], cot_comp[0]
    rows, width = segment.shape
    seg = rows * blocks
    past = KEYS - seg
    heads = H // blocks
    cols = heads * DH
    core, near, blk, rest = axis_bits()

    def my_cols(weight):
        return lax.dynamic_slice_in_dim(weight, here * cols, cols, 1)

    far = [swap(value, "blk") for value in (segment, memory, comp_memory)]

    windows = memory.reshape(memory.shape[0] // RATE, RATE * width)
    new_compressed = (matmul(windows, w_comp) + b_comp.astype(wide)).astype(narrow)
    grad_w_comp = outer(windows, cot_comp).astype(narrow)
    grad_b_comp = jnp.sum(cot_comp.astype(wide), 0)

    sinus = sinus_table()
    relative = matmul(sinus, my_cols(w_rel)).astype(narrow)
    w_query_mine = my_cols(w_query)
    w_kv = jnp.stack(
        [my_cols(w_key).reshape(width, heads, DH), my_cols(w_value).reshape(width, heads, DH)], 2
    ).reshape(width, 2 * cols)

    keys_in = jnp.concatenate(
        [
            in_order(here, comp_memory, far[2]),
            in_order(here, memory, far[1]),
            in_order(here, segment, far[0]),
        ],
        0,
    )
    normal, inverse = moments(keys_in.astype(wide))
    normed = (normal * first_gain.astype(wide) + first_bias.astype(wide)).astype(narrow)
    seg_normed = normed[past:]
    query_rows = matmul(seg_normed, w_query_mine)
    u_mine = lax.dynamic_slice_in_dim(u_bias, here * cols, cols, 0).astype(wide)
    v_mine = lax.dynamic_slice_in_dim(v_bias, here * cols, cols, 0).astype(wide)
    q_content = (query_rows + u_mine).astype(narrow)
    q_position = (query_rows + v_mine).astype(narrow)
    key_value = matmul(normed, w_kv).astype(narrow)
    attended_heads, probs = attend(mem_start, q_content, q_position, key_value, relative)

    ours = lax.dynamic_slice_in_dim(attended_heads, here * rows, rows, 0)
    theirs = lax.dynamic_slice_in_dim(attended_heads, (1 - here) * rows, rows, 0)
    attended = in_order(here, ours, swap(theirs, "blk"), 1)
    hidden = segment.astype(wide) + matmul(attended, w_out)
    normal_second, inverse_second = moments(hidden)
    second_normed = (
        normal_second * second_gain.astype(wide) + second_bias.astype(wide)
    ).astype(narrow)
    pre_gelu = matmul(second_normed, w_up) + b_up.astype(wide)
    gelu_wide, gelu_back = jax.vjp(partial(jax.nn.gelu, approximate=True), pre_gelu)
    gelu_out = gelu_wide.astype(narrow)
    layer_out = (hidden + matmul(gelu_out, w_down) + b_down.astype(wide)).astype(narrow)

    cot_wide = cot_out.astype(wide)
    d_pre = gelu_back(back_through(cot_out, w_down))[0].astype(narrow)
    d_second = back_through(d_pre, w_up)
    d_hidden = cot_wide + norm_back(
        d_second, normal_second, inverse_second, second_gain.astype(wide)
    )
    d_branch = d_hidden.astype(narrow)
    d_rows = back_through(d_branch, w_out).astype(narrow)
    ours = lax.dynamic_slice_in_dim(d_rows, here * cols, cols, 1)
    theirs = lax.dynamic_slice_in_dim(d_rows, (1 - here) * cols, cols, 1)
    d_attended = in_order(here, ours, swap(theirs, "blk"), 0)
    grad_b_down = jnp.sum(cot_wide, 0)
    grad_b_up = jnp.sum(d_pre.astype(wide), 0)
    grad_second_gain = jnp.sum(d_second * normal_second, 0)
    grad_second_bias = jnp.sum(d_second, 0)
    grad_w_down = outer(gelu_out, cot_out).astype(narrow)
    grad_w_up = outer(second_normed, d_pre).astype(narrow)
    grad_w_out = outer(attended, d_branch).astype(narrow)

    d_query, d_kv, d_relative, grad_u, grad_v = attend_back(
        probs, q_content, q_position, key_value, relative, d_attended
    )
    d_normed = back_through(d_kv[past:], w_kv) + back_through(d_query, w_query_mine)
    ours = lax.dynamic_slice_in_dim(d_normed, here * rows, rows, 0)
    theirs = lax.dynamic_slice_in_dim(d_normed, (1 - here) * rows, rows, 0).astype(narrow)
    d_normed_rows = ours + swap(theirs, "blk").astype(wide)
    normal_rows, inverse_rows = moments(segment.astype(wide))
    d_segment = (
        d_hidden + norm_back(d_normed_rows, normal_rows, inverse_rows, first_gain.astype(wide))
    ).astype(narrow)
    grad_w_kv = outer(normed, d_kv)
    grad_w_query = outer(seg_normed, d_query)
    grad_w_rel = outer(sinus, d_relative)

    def norm_sums(weight, grad, d_heads):
        column_sums = jnp.sum(d_heads.astype(wide), 0)
        weight = weight.astype(wide)
        by_bias = jnp.sum(weight * column_sums[None, :], 1)
        return jnp.sum(weight * grad, 1), by_bias

    kv_gain, kv_bias = norm_sums(w_kv, grad_w_kv, d_kv)
    q_gain, q_bias = norm_sums(w_query_mine, grad_w_query, d_query)
    grad_first_bias = kv_bias + q_bias
    grad_first_gain = (
        kv_gain + q_gain - first_bias.astype(wide) * grad_first_bias
    ) / first_gain.astype(wide)

    def spread(vector):
        return lax.dynamic_update_slice_in_dim(
            jnp.zeros((width,), wide), vector.reshape(cols), here * cols, 0
        )

    vectors = [
        grad_first_gain,
        grad_first_bias,
        spread(grad_u),
        spread(grad_v),
        grad_second_gain,
        grad_second_bias,
        grad_b_up,
        grad_b_down,
        grad_b_comp,
    ]
    total = sum_over_all(jnp.concatenate(vectors).reshape(-1, 128)).reshape(-1)
    split = []
    at = 0
    for vector in vectors:
        split.append(total[at : at + vector.shape[0]])
        at += vector.shape[0]

    x_first = core + near + blk + rest
    y_first = core + blk + rest + near
    z_first = core + rest + near + blk

    def reduced(value, steps):
        return gather_back(scatter_sum(value, steps), steps).astype(wide)

    full_comp = reduced(grad_w_comp, x_first)
    full_up = reduced(grad_w_up, x_first)
    full_down = reduced(grad_w_down, z_first)
    full_out = reduced(grad_w_out, y_first)

    def reduced_heads(value, steps):
        value = scatter_sum(value.astype(narrow), steps)
        value = jnp.stack([value, swap(value, "blk")], 0)
        value = jnp.where(here == 0, value, value[::-1])
        value = jnp.moveaxis(value, 0, 1)
        return gather_back(value, steps)

    kv = reduced_heads(grad_w_kv, core + near + rest).astype(wide)
    kv = kv.reshape(width, blocks, heads, 2, DH)
    full_key = kv[:, :, :, 0].reshape(width, width)
    full_value = kv[:, :, :, 1].reshape(width, width)
    pair = jnp.concatenate([grad_w_query, grad_w_rel], 1)
    pair = reduced_heads(pair, core + rest + near).astype(wide).reshape(width, blocks, 2, cols)
    full_query = pair[:, :, 0].reshape(width, width)
    full_rel = pair[:, :, 1].reshape(width, width)

    return (
        layer_out[None],
        d_segment[None],
        new_compressed[None],
        split[0],
        split[1],
        full_query,
        full_key,
        full_value,
        full_rel,
        split[2],
        split[3],
        full_out,
        split[4],
        split[5],
        full_up,
        split[6],
        full_down,
        split[7],
        full_comp,
        split[8],
    )


def solution(mesh):
    rows = P("dp", "blk", None)
    in_specs = (rows,) * 3 + (P("dp"),) + (P(),) * 17 + (rows,) * 2
    out_specs = (rows,) * 3 + (P(),) * 17
    return jax.shard_map(
        on_device, mesh=mesh, in_specs=in_specs, out_specs=out_specs, check_vma=False
    )
```

```python
from functools import partial

import jax
import jax.numpy as jnp
from jax import lax
from jax.experimental import pallas as pl
from jax.experimental.pallas import tpu as pltpu
from jax.sharding import PartitionSpec as P

D = 1024
H = 8
DH = 128
FF = 4096
CMEM = 512
RATE = 3
KEYS = 2432

TILE = 192
FF_TILE = 512
epsilon = 1e-05
negative = -1e30
wide = jnp.float32
narrow = jnp.bfloat16
MIB = 1 << 20


def dot(left, right, left_dim, right_dim):
    return lax.dot_general(
        left, right, (((left_dim,), (right_dim,)), ((), ())), preferred_element_type=wide
    )


def shape(rows, cols, dtype=narrow):
    return jax.ShapeDtypeStruct((rows, cols), dtype)


def whole(rows, cols):
    return pl.BlockSpec((rows, cols), lambda *_: (0, 0))


class Order:
    def __init__(self):
        self.last = []

    def call(self, kernel, name, scalars, arrays, grid, in_specs, out_specs, out_shape, scratch=(), after=(), aliases=()):
        count = len(arrays)
        after = list(after) + self.last

        def body(scalar_ref, *refs):
            kernel(scalar_ref, *refs[:count], *refs[count + len(after) :])

        out = pl.pallas_call(
            body,
            grid_spec=pltpu.PrefetchScalarGridSpec(
                num_scalar_prefetch=1,
                grid=grid,
                in_specs=list(in_specs) + [pl.BlockSpec(memory_space=pl.ANY)] * len(after),
                out_specs=out_specs,
                scratch_shapes=list(scratch),
            ),
            out_shape=out_shape,
            input_output_aliases={1 + i: o for i, o in aliases},
            compiler_params=pltpu.CompilerParams(vmem_limit_bytes=60 * MIB),
            cost_estimate=pl.CostEstimate(
                flops=1000, bytes_accessed=1000, transcendentals=0
            ),
            name=name,
        )(jnp.stack([jnp.asarray(s, jnp.int32) for s in scalars]), *arrays, *after)
        self.last = [out[-1] if isinstance(out, (list, tuple)) else out]
        return out


def swap(value, axis, bit=0):
    pairs = [(source, source ^ (1 << bit)) for source in range(lax.axis_size(axis))]
    return lax.ppermute(value, axis, pairs)


def side(axis, bit=0):
    return (lax.axis_index(axis) >> bit) & 1


def place_of(steps):
    place = jnp.int32(0)
    for axis, bit in steps:
        place = place * 2 + side(axis, bit)
    return place


def add_split(order, chains, steps, name):
    in_specs, out_specs, out_shape, arrays = [], [], [], []
    for number, (kept, received, _) in enumerate(chains):
        rows, cols = kept.shape
        block = rows // 2 // steps
        theirs = pl.BlockSpec((block, cols), lambda i, ids, n=number: ((1 - ids[n]) * steps + i, 0))
        ours = pl.BlockSpec((block, cols), lambda i, ids, n=number: (ids[n] * steps + i, 0))
        arrays += [kept, received, kept, received]
        in_specs += [theirs, theirs, ours, ours]
        out_specs += [pl.BlockSpec((block, cols), lambda i, ids: (i, 0))] * 2
        out_shape += [shape(rows // 2, cols)] * 2

    def kernel(ids, *refs):
        ins, outs = refs[: 4 * len(chains)], refs[4 * len(chains) :]
        for number, out in enumerate(outs):
            a, b = ins[2 * number], ins[2 * number + 1]
            out[...] = (a[...].astype(wide) + b[...].astype(wide)).astype(narrow)

    out = order.call(kernel, name, [c[2] for c in chains], arrays, (steps,), in_specs, out_specs, out_shape)
    return [(out[2 * n], out[2 * n + 1]) for n in range(len(chains))]


def add(order, pairs, name):
    arrays = [value for pair in pairs for value in pair]

    def kernel(ids, *refs):
        for number, out in enumerate(refs[len(arrays) :]):
            a, b = refs[2 * number], refs[2 * number + 1]
            out[...] = (a[...].astype(wide) + b[...].astype(wide)).astype(narrow)

    return order.call(
        kernel,
        name,
        [0],
        arrays,
        (1,),
        [whole(*a.shape) for a in arrays],
        [whole(*a.shape) for a, _ in pairs],
        [shape(*a.shape) for a, _ in pairs],
    )


def gate(order, *values):
    place = pl.BlockSpec(memory_space=pl.ANY)
    out = order.call(
        lambda ids, *refs: None,
        "gate",
        [0],
        values,
        (1,),
        [place] * len(values),
        [place] * len(values),
        [jax.ShapeDtypeStruct(value.shape, value.dtype) for value in values],
        aliases=[(n, n) for n in range(len(values))],
    )
    return out[0] if len(values) == 1 else out


class Scatter:
    def __init__(self, order, name, chains):
        self.order, self.name = order, name
        self.steps = [steps for _, _, steps in chains]
        self.keep = [keep for _, keep, _ in chains]
        self.received = [swap(send, *steps[0]) for send, _, steps in chains]
        self.at = 0

    def step(self, blocks=1):
        self.at += 1
        if self.at == len(self.steps[0]):
            self.keep = add(self.order, list(zip(self.keep, self.received)), self.name)
            return self.keep
        chains = [
            (keep, received, side(*steps[self.at]))
            for keep, received, steps in zip(self.keep, self.received, self.steps)
        ]
        halves = add_split(self.order, chains, blocks, self.name)
        self.keep = [keep for _, keep in halves]
        self.received = [swap(send, *steps[self.at]) for (send, _), steps in zip(halves, self.steps)]


def join(order, pairs, name):
    arrays = [value for pair in pairs for value in pair]

    def kernel(ids, *refs):
        for number, out in enumerate(refs[len(arrays) :]):
            a, b = refs[2 * number], refs[2 * number + 1]
            rows = a.shape[0]
            out[0:rows, :] = a[...]
            out[rows:, :] = b[...]

    outs = [(2 * a.shape[0], a.shape[1]) for a, _ in pairs]
    return order.call(
        kernel,
        name,
        [0],
        arrays,
        (1,),
        [whole(*a.shape) for a in arrays],
        [whole(*out) for out in outs],
        [shape(*out) for out in outs],
    )


class Gather:
    def __init__(self, order, name, chains):
        self.order, self.name = order, name
        self.values = [value for value, _ in chains]
        self.steps = [list(steps) for _, steps in chains]
        self.send()

    def send(self):
        self.received = [swap(value, *steps.pop()) for value, steps in zip(self.values, self.steps)]

    def step(self):
        self.values = join(self.order, list(zip(self.values, self.received)), self.name)
        if self.steps[0]:
            self.send()


def two_pieces(value, first):
    return [value, swap(value, *first)]


def four_pieces(value, first, second):
    beside = swap(value, *second)
    return [value, beside, swap(value, *first), swap(beside, *first)]


def assemble(order, pieces, blocks, places, outs, out_block, index, inside, splits, name):
    rows, cols = pieces[0].shape
    chunk, part = rows // blocks, cols // splits
    count = len(pieces)

    def kernel(ids, *refs):
        ins, out_refs = refs[:count], refs[count:]
        piece = pl.program_id(0)

        def copy(ref, out):
            for r in range(blocks):
                row, col = inside(r ^ ids[1])
                out[pl.ds(pl.multiple_of(row, 8), chunk), pl.ds(pl.multiple_of(col, 128), part)] = ref[
                    r * chunk : (r + 1) * chunk, :
                ].astype(wide)

        for p, ref in enumerate(ins):
            for o, out in enumerate(out_refs):
                here = piece == p
                if len(out_refs) > 1:
                    here = here & ((p ^ ids[0]) == o)
                pl.when(here)(partial(copy, ref, out))

    def piece_spec(p):
        return pl.BlockSpec(
            (rows, part), lambda i, j, ids: (0, jnp.where(i == p, j, jnp.where(i < p, 0, splits - 1)))
        )

    return order.call(
        kernel,
        name,
        places,
        pieces,
        (count, splits),
        [piece_spec(p) for p in range(count)],
        [pl.BlockSpec(out_block, lambda i, j, ids: index(i ^ ids[0], j))] * len(outs),
        [shape(*out, wide) for out in outs],
    )


def widen(order, value, name):
    rows, cols = value.shape
    steps = 4

    def kernel(ids, ref, out):
        out[...] = ref[...].astype(wide)

    at = pl.BlockSpec((rows // steps, cols), lambda i, ids: (i, 0))
    return order.call(kernel, name, [0], [value], (steps,), [at], at, shape(rows, cols, wide))


def widen_heads(order, gathered, chunk, extra, width, cols, name):
    arrays = 4
    rows = gathered.shape[0] // arrays
    count = rows // (chunk + extra)

    def kernel(ids, ref, *outs):
        def copy(out):
            for r in range(count):
                at = r * (chunk + extra)
                row, col = r // 2 * chunk, r % 2 * cols
                out[row : row + chunk, col : col + cols] = ref[at : at + chunk, :].astype(wide)

        for number, out in enumerate(outs):
            pl.when(pl.program_id(0) == number)(partial(copy, out))

    return order.call(
        kernel,
        name,
        [0],
        [gathered],
        (arrays,),
        [pl.BlockSpec((rows, cols), lambda i, ids: (i, 0))],
        [whole(width, width)] * arrays,
        [shape(width, width, wide)] * arrays,
    )


def project_kernel(count, lengths, ids, *refs):
    parts, (gain, bias, wq, wk, wv), outs = refs[:count], refs[count : count + 5], refs[count + 5 :]
    if count < len(lengths):
        firsts = [sum(lengths[:n]) for n in range(len(lengths))]
        parts = [parts[0].at[first : first + length, :] for first, length in zip(firsts, lengths)]
        count = len(lengths)
    for number, part in enumerate(parts):
        normed, k, v = outs[3 * number : 3 * number + 3]
        values = part[...].astype(wide)
        centred = values - jnp.mean(values, -1, keepdims=True)
        inverse = lax.rsqrt(jnp.mean(centred * centred, -1, keepdims=True) + epsilon)
        low = (centred * inverse * gain[...].astype(wide) + bias[...].astype(wide)).astype(narrow)
        normed[...] = low
        k[...] = dot(low, wk[...], 1, 0).astype(narrow)
        v[...] = dot(low, wv[...], 1, 0).astype(narrow)
        if number == 0 and len(outs) > 3 * count:
            outs[-1][...] = dot(low, wq[...], 1, 0)


def project(order, here, parts, lengths, query, weights, cols, after=()):
    gain, bias, wq, wk, wv = weights
    width = wq.shape[0]
    weight = pl.BlockSpec((width, cols), lambda i, ids: (0, ids[0]))
    unused = whole(16, 128)
    out_shape = [s for n in lengths for s in (shape(n, width), shape(n, cols), shape(n, cols))]
    if query:
        out_shape.append(shape(lengths[0], cols, wide))
    out = order.call(
        partial(project_kernel, len(parts), lengths),
        "project",
        [here],
        list(parts) + [gain[None], bias[None], wq, wk, wv],
        (1,),
        [whole(*p.shape) for p in parts] + [whole(1, width)] * 2 + [weight if query else unused, weight, weight],
        [whole(*o.shape) for o in out_shape],
        out_shape,
        after=after,
    )
    triples = [tuple(out[3 * n : 3 * n + 3]) for n in range(len(lengths))]
    return triples + ([out[-1]] if query else [])


def tiles_of(seg, keys, tile):
    tiles = []
    for first in range(0, seg, tile):
        used = keys - seg + first + tile
        cols = -(-used // 128) * 128
        tiles.append((first, cols, keys - cols, cols - used))
    return tiles


def unskew(grid, tile, cols, pad):
    parts = []
    for group in range(tile // 8):
        shift = tile - 1 + pad - 8 * group - 7
        rows = grid[8 * group : 8 * group + 8]
        parts.append(pltpu.roll(rows, shift, 1) if shift else rows)
    moved = jnp.concatenate(parts, 0)
    left = 7 - (lax.broadcasted_iota(jnp.int32, (tile, cols), 0) & 7)
    for bit in range(3):
        moved = jnp.where((left & (1 << bit)) != 0, pltpu.roll(moved, 1 << bit, 1), moved)
    return moved


def spans(parts, here):
    out = []
    at = 0
    for length in parts:
        own = pl.multiple_of(2 * at + here * length, 16)
        far = pl.multiple_of(2 * at + (1 - here) * length, 16)
        out.append((pl.ds(at, length), pl.ds(own, length), pl.ds(far, length)))
        at += length
    return out


def place_parts(parts, here, own, far, out):
    for (_, own_rows, far_rows), own_part, far_part in zip(spans(parts, here), own, far):
        out[own_rows, :] = own_part[...]
        out[far_rows, :] = far_part[...]


def place_queries(parts, here, q_own, q_far, u, v, qc, qp):
    ((_, own_rows, far_rows),) = spans(parts[2:], here)
    for ref, rows in ((q_own, own_rows), (q_far, far_rows)):
        qc[rows, :] = (ref[...] + u[...].astype(wide)).astype(narrow)
        qp[rows, :] = (ref[...] + v[...].astype(wide)).astype(narrow)


def attend_kernel(parts, ids, q_own, q_far, u, v, *refs):
    k_own, k_far, v_own, v_far = refs[0:3], refs[3:6], refs[6:9], refs[9:12]
    rel, out_own, out_far, probs_ref, qc, qp, ks, vs, outs = refs[12:]
    here, start = ids[0], ids[1]
    place_queries(parts, here, q_own, q_far, u, v, qc, qp)
    place_parts(parts, here, k_own, k_far, ks)
    place_parts(parts, here, v_own, v_far, vs)
    seg, keys = qc.shape[0], ks.shape[0]
    past = keys - seg
    factor = DH**-0.5 * 1.4426950408889634
    for first, cols, base, pad in tiles_of(seg, keys, TILE):
        rows = pl.ds(first, TILE)
        content = dot(qc[rows, :], ks[0:cols, :], 1, 1)
        table = dot(qp[rows, :], rel[base : base + cols, :], 1, 1)
        table = pltpu.roll(table, cols - (TILE - 1 + pad), 1, stride=1, stride_axis=0)
        scores = content + table
        left = scores[:, :CMEM]
        lane = lax.broadcasted_iota(jnp.int32, left.shape, 1)
        left = jnp.where(lane >= start, left, negative)
        edge = (past + first) // 128 * 128
        right = scores[:, edge:]
        lane = lax.broadcasted_iota(jnp.int32, right.shape, 1) + (edge - past - first)
        row = lax.broadcasted_iota(jnp.int32, right.shape, 0)
        right = jnp.where(lane <= row, right, negative)
        scores = jnp.concatenate([left, scores[:, CMEM:edge], right], 1)
        largest = jnp.max(scores, -1, keepdims=True)
        probs = jnp.exp2(scores * factor - largest * factor)
        probs = (probs * (1.0 / jnp.sum(probs, -1, keepdims=True))).astype(narrow)
        probs_ref[0, rows, 0:cols] = probs
        outs[rows, :] = dot(probs, vs[0:cols, :], 1, 0).astype(narrow)
    ((_, own_rows, far_rows),) = spans(parts[2:], here)
    out_own[...] = outs[own_rows, :]
    out_far[...] = outs[far_rows, :]


def part_specs(parts, first):
    return [pl.BlockSpec((length, DH), lambda h, ids: (0, h + first)) for length in parts]


def attend(order, here, start, parts, inputs, first, heads):
    q_own, q_far, u, v, k_own, k_far, v_own, v_far, rel = inputs
    rows, keys = parts[2], rel.shape[0]
    query = pl.BlockSpec((rows, DH), lambda h, ids: (0, h + first))
    bias = pl.BlockSpec((1, DH), lambda h, ids: (0, h + first + ids[0] * (H // 2)))
    out = pl.BlockSpec((rows, DH), lambda h, ids: (0, h))
    seg = 2 * rows
    return order.call(
        partial(attend_kernel, parts),
        "attend",
        [here, start],
        [q_own, q_far, u[None], v[None], *k_own, *k_far, *v_own, *v_far, rel],
        (heads,),
        [query, query, bias, bias]
        + part_specs(parts, first) * 4
        + [pl.BlockSpec((keys, DH), lambda h, ids: (0, h + first))],
        [out, out, pl.BlockSpec((1, seg, keys), lambda h, ids: (h, 0, 0))],
        [shape(rows, heads * DH)] * 2 + [jax.ShapeDtypeStruct((heads, seg, keys), narrow)],
        [pltpu.VMEM((seg, DH), narrow)] * 2
        + [pltpu.VMEM((keys, DH), narrow)] * 2
        + [pltpu.VMEM((seg, DH), narrow)],
    )


def attend_back_kernel(parts, ids, probs_ref, q_own, q_far, u, v, *refs):
    k_own, k_far, v_own, v_far = refs[0:3], refs[3:6], refs[6:9], refs[9:12]
    rel, da_own, da_far, dq_own, dq_far, dk_ref, dv_ref, drel_ref, gu_ref, gv_ref = refs[12:22]
    qc_ref, qp_ref, ks, vs, das, dqs, stage, key_sum, value_sum, rel_sum = refs[22:]
    here = ids[0]
    place_queries(parts, here, q_own, q_far, u, v, qc_ref, qp_ref)
    place_parts(parts, here, k_own, k_far, ks)
    place_parts(parts, here, v_own, v_far, vs)
    ((_, own_rows, far_rows),) = spans(parts[2:], here)
    das[own_rows, :] = da_own[...]
    das[far_rows, :] = da_far[...]
    seg, keys = qc_ref.shape[0], ks.shape[0]
    scale = DH**-0.5

    grad_u = jnp.zeros((1, DH), wide)
    grad_v = jnp.zeros((1, DH), wide)
    for step, (first, cols, base, pad) in enumerate(tiles_of(seg, keys, TILE)[::-1]):
        rows = pl.ds(first, TILE)
        probs = probs_ref[0, rows, 0:cols]
        probs_wide = probs.astype(wide)
        d_out, qc, qp = das[rows, :], qc_ref[rows, :], qp_ref[rows, :]
        d_probs = dot(d_out, vs[0:cols, :], 1, 1)
        weighted = probs_wide * d_probs
        d_scores = weighted - probs_wide * jnp.sum(weighted, -1, keepdims=True)
        d_low = d_scores.astype(narrow)
        d_table = unskew(d_scores, TILE, cols, pad).astype(narrow)
        d_content = dot(d_low, ks[0:cols, :], 1, 0)
        d_position = dot(d_table, rel[base : base + cols, :], 1, 0)
        grad_u += jnp.sum(d_content, 0, keepdims=True)
        grad_v += jnp.sum(d_position, 0, keepdims=True)
        dqs[rows, :] = ((d_content + d_position) * scale).astype(narrow)
        d_key = dot(qc, d_low, 0, 0)
        d_value = dot(d_out, probs, 0, 0)
        d_rel = dot(qp, d_table, 0, 0)
        if step == 0:
            key_sum[...] = d_key
            value_sum[...] = d_value
            rel_sum[...] = d_rel
        else:
            key_sum[:, 0:cols] += d_key
            value_sum[:, 0:cols] += d_value
            rel_sum[:, base : base + cols] += d_rel
    gu_ref[...] = grad_u * scale
    gv_ref[...] = grad_v * scale
    drel_ref[...] = (rel_sum[...] * scale).T.astype(narrow)
    dq_own[...] = dqs[own_rows, :]
    dq_far[...] = dqs[far_rows, :]
    block = sum(parts)
    for total, factor, out in ((key_sum, scale, dk_ref), (value_sum, 1.0, dv_ref)):
        stage[...] = (total[...] * factor).T.astype(narrow)
        for rows, mine, theirs in spans(parts, here):
            out[rows, :] = stage[mine, :]
            out[pl.ds(block + rows.start, rows.size), :] = stage[theirs, :]


def attend_back(order, here, parts, probs, inputs, da_own, da_far, first, heads):
    q_own, q_far, u, v, k_own, k_far, v_own, v_far, rel = inputs
    rows, keys = parts[2], rel.shape[0]
    seg = 2 * rows
    query = pl.BlockSpec((rows, DH), lambda h, ids: (0, h + first))
    bias = pl.BlockSpec((1, DH), lambda h, ids: (0, h + first + ids[0] * (H // 2)))
    key = pl.BlockSpec((keys, DH), lambda h, ids: (0, h + first))
    query_out = pl.BlockSpec((rows, DH), lambda h, ids: (0, h))
    key_out = pl.BlockSpec((keys, DH), lambda h, ids: (0, h))
    per_head = pl.BlockSpec((1, DH), lambda h, ids: (0, h))
    small, large = pltpu.VMEM((seg, DH), narrow), pltpu.VMEM((keys, DH), narrow)
    return order.call(
        partial(attend_back_kernel, parts),
        "attend_back",
        [here],
        [probs, q_own, q_far, u[None], v[None], *k_own, *k_far, *v_own, *v_far, rel, da_own, da_far],
        (heads,),
        [pl.BlockSpec((1, seg, keys), lambda h, ids: (h, 0, 0)), query, query, bias, bias]
        + part_specs(parts, first) * 4
        + [key, query, query],
        [query_out, query_out, key_out, key_out, key_out, per_head, per_head],
        [shape(rows, heads * DH)] * 2
        + [shape(keys, heads * DH)] * 3
        + [shape(1, heads * DH, wide)] * 2,
        [small, small, large, large, small, small, large] + [pltpu.VMEM((DH, keys), wide)] * 3,
    )


def middle_kernel(own_pieces, far_pieces, ids, *refs):
    mine, refs = refs[:own_pieces], refs[own_pieces:]
    received, refs = refs[:far_pieces], refs[far_pieces:]
    segment, cot, w_out, gain, bias, w_up, b_up, w_down, b_down = refs[:9]
    (layer_out, packed, att_keep, gelu_theirs, gelu_mine, d_theirs, d_mine, d_hidden, da_mine, da_theirs, g_up, g_gain, g_bias, g_down,
     normal, inverse, layer, back) = refs[9:]
    normed, d_branch, att_send = packed.at[:, 0:D], packed.at[:, D : 2 * D], packed.at[:, 2 * D :]
    step = pl.program_id(0)
    steps = pl.num_programs(0)
    here = ids[0]
    half = D // 2

    @pl.when(step == 0)
    def _():
        own = jnp.concatenate([ref[...] for ref in mine], 1)
        far = jnp.concatenate([ref[...] for ref in received], 1)
        own_rows = pl.ds(pl.multiple_of(here * half, 128), half)
        far_rows = pl.ds(pl.multiple_of((1 - here) * half, 128), half)
        hidden = segment[...].astype(wide) + dot(own, w_out[own_rows, :], 1, 0) + dot(far, w_out[far_rows, :], 1, 0)
        same = here == ids[1]
        att_keep[...] = jnp.where(same, own, far)
        att_send[...] = jnp.where(same, far, own)
        centred = hidden - jnp.mean(hidden, -1, keepdims=True)
        scale = lax.rsqrt(jnp.mean(centred * centred, -1, keepdims=True) + epsilon)
        inverse[...] = scale
        normal[...] = centred * scale
        normed[...] = (normal[...] * gain[...].astype(wide) + bias[...].astype(wide)).astype(narrow)
        layer[...] = hidden + b_down[...].astype(wide)
        back[...] = jnp.zeros_like(back)

    t = dot(normed[...], w_up[...], 1, 0) + b_up[...].astype(wide)
    d_gelu = dot(cot[...], w_down[...], 1, 1)
    square = t * t
    slope = 0.7978845608028654
    bent = jnp.tanh(slope * t * (1.0 + 0.044715 * square))
    rise = 0.5 * (1.0 + bent)
    gelu = (t * rise).astype(narrow)
    change = rise + (0.5 * slope) * t * (1.0 - bent * bent) * (1.0 + (3 * 0.044715) * square)
    d_pre = (d_gelu * change).astype(narrow)
    layer[...] += dot(gelu, w_down[...], 1, 0)
    back[...] += dot(d_pre, w_up[...], 1, 1)
    g_up[...] = jnp.sum(d_pre.astype(wide), 0, keepdims=True)

    @pl.when(step < steps // 2)
    def _():
        gelu_theirs[...] = gelu
        d_theirs[...] = d_pre

    @pl.when(step >= steps // 2)
    def _():
        gelu_mine[...] = gelu
        d_mine[...] = d_pre

    @pl.when(step == steps - 1)
    def _():
        layer_out[...] = layer[...].astype(narrow)
        e, n = back[...], normal[...]
        cot_wide = cot[...].astype(wide)
        en = e * n
        g_gain[...] = jnp.sum(en, 0, keepdims=True)
        g_bias[...] = jnp.sum(e, 0, keepdims=True)
        g_down[...] = jnp.sum(cot_wide, 0, keepdims=True)
        by = gain[...].astype(wide)
        inner = e * by - jnp.mean(e * by, -1, keepdims=True) - n * jnp.mean(en * by, -1, keepdims=True)
        d_wide = cot_wide + inner * inverse[...]
        d_hidden[...] = d_wide
        low = d_wide.astype(narrow)
        d_branch[...] = low
        own_rows = pl.ds(pl.multiple_of(here * half, 128), half)
        far_rows = pl.ds(pl.multiple_of((1 - here) * half, 128), half)
        da_theirs[...] = dot(low, w_out[far_rows, :], 1, 1).astype(narrow)
        da_mine[...] = dot(low, w_out[own_rows, :], 1, 1).astype(narrow)


def middle(order, here, core, mine, received, segment, cot, w_out, gain, bias, w_up, b_up, w_down, b_down):
    rows, width = segment.shape
    units = w_up.shape[1]
    steps = units // FF_TILE
    half = steps // 2

    def tile(j, ids):
        return jnp.where(j < half, (1 - ids[1]) * half + j, ids[1] * half + j - half)

    up = pl.BlockSpec((width, FF_TILE), lambda j, ids: (0, tile(j, ids)))
    down = pl.BlockSpec((FF_TILE, width), lambda j, ids: (tile(j, ids), 0))
    unit = pl.BlockSpec((1, FF_TILE), lambda j, ids: (0, tile(j, ids)))
    theirs = pl.BlockSpec((rows, FF_TILE), lambda j, ids: (0, jnp.minimum(j, half - 1)))
    ours = pl.BlockSpec((rows, FF_TILE), lambda j, ids: (0, jnp.maximum(j - half, 0)))
    row, vector = whole(rows, width), whole(1, width)
    heads = whole(rows, width // 2)
    return order.call(
        partial(middle_kernel, len(mine), len(received)),
        "middle",
        [here, core],
        list(mine) + list(received) + [segment, cot, w_out, gain[None], bias[None], w_up, b_up[None], w_down, b_down[None]],
        (steps,),
        [whole(*a.shape) for a in list(mine) + list(received)]
        + [row, row, whole(width, width), vector, vector, up, unit, down, vector],
        [row, whole(rows, 5 * width // 2), heads, theirs, ours, theirs, ours, row, heads, heads, unit]
        + [vector] * 3,
        [shape(rows, width), shape(rows, 5 * width // 2), shape(rows, width // 2)]
        + [shape(rows, units // 2)] * 4
        + [shape(rows, width, wide)]
        + [shape(rows, width // 2)] * 2
        + [shape(1, units, wide)]
        + [shape(1, width, wide)] * 3,
        [pltpu.VMEM((rows, width), wide), pltpu.VMEM((rows, 1), wide)] + [pltpu.VMEM((rows, width), wide)] * 2,
    )


def outer_pair(order, l_own, l_far, r_own, r_far, which, name, after=()):
    count, units, cols = l_own[0].shape[0], l_own[2], r_own[2]
    rows = units // 2
    block = 256 if rows % 256 == 0 else rows
    steps = rows // block

    def kernel(ids, lo, lf, ro, rf, out):
        out[...] = (dot(lo[...], ro[...], 0, 0) + dot(lf[...], rf[...], 0, 0)).astype(narrow)

    def left(first):
        return pl.BlockSpec((count, block), lambda i, ids: (0, first // block + ids[0] * steps + i))

    def right(first):
        return pl.BlockSpec((count, cols), lambda i, ids: (0, first // cols))

    return order.call(
        kernel,
        name,
        [which],
        [l_own[0], l_far[0], r_own[0], r_far[0]],
        (steps,),
        [left(l_own[1]), left(l_far[1]), right(r_own[1]), right(r_far[1])],
        pl.BlockSpec((block, cols), lambda i, ids: (i, 0)),
        shape(rows, cols),
        after=after,
    )


def segment_back_kernel(count, block, ids, *refs):
    dq_own, dq_far, dk, dv = (refs[n * count : (n + 1) * count] for n in range(4))
    wq, wk, wv, own, far = refs[4 * count :]
    rows = dq_own[0].shape[0]

    def through(dq, last):
        at = pl.ds(last - rows, rows)
        total = dot(jnp.concatenate([d[...] for d in dq], 1), wq[...], 1, 1)
        total += dot(jnp.concatenate([d[at, :] for d in dk], 1), wk[...], 1, 1)
        return total + dot(jnp.concatenate([d[at, :] for d in dv], 1), wv[...], 1, 1)

    far[...] = through(dq_far, 2 * block).astype(narrow)
    own[...] = through(dq_own, block)


def segment_back(order, here, dq_own, dq_far, dk, dv, wq, wk, wv, block):
    rows, width, cols = dq_own[0].shape[0], wq.shape[0], wq.shape[1] // 2
    weight = pl.BlockSpec((width, cols), lambda i, ids: (0, ids[0]))
    arrays = [*dq_own, *dq_far, *dk, *dv]
    return order.call(
        partial(segment_back_kernel, len(dk), block),
        "segment_back",
        [here],
        arrays + [wq, wk, wv],
        (1,),
        [whole(*a.shape) for a in arrays] + [weight] * 3,
        [whole(rows, width)] * 2,
        [shape(rows, width, wide), shape(rows, width)],
    )


def grad_heads_kernel(parts, count, chunk, extra, ids, *refs):
    normed, refs = refs[:6], refs[6:]
    sinus, refs = refs[0], refs[1:]
    dq_own, dq_far, dk, dv, drel = (refs[n * count : (n + 1) * count] for n in range(5))
    wq, wk, wv, out, by_gain, by_bias = refs[5 * count :]
    param = pl.program_id(0)

    @pl.when(param == 0)
    def _():
        by_gain[...] = jnp.zeros_like(by_gain)
        by_bias[...] = jnp.zeros_like(by_bias)

    def store(grad):
        for n in range(grad.shape[0] // chunk):
            at = n * (chunk + extra)
            out[at : at + chunk, :] = grad[n * chunk : (n + 1) * chunk, :].astype(narrow)
            out[at + chunk : at + chunk + extra, :] = jnp.zeros((extra, grad.shape[1]), narrow)

    def sums(weight, grad, d_heads):
        weight = weight[...].astype(wide)
        column = sum(jnp.sum(d.astype(wide), 0, keepdims=True) for d in d_heads)
        by_gain[...] += jnp.sum(weight * grad, 1, keepdims=True)
        by_bias[...] += jnp.sum(weight * column, 1, keepdims=True)

    def beside(refs, rows=slice(None)):
        return jnp.concatenate([ref[rows, :] for ref in refs], 1)

    @pl.when(param == 0)
    def _():
        own, far = beside(dq_own), beside(dq_far)
        grad = (dot(own, normed[2][...], 0, 0) + dot(far, normed[5][...], 0, 0)).T
        store(grad)
        sums(wq, grad, (own, far))

    for number, weight, d_heads in ((1, wk, dk), (2, wv, dv)):

        @pl.when(param == number)
        def _(weight=weight, d_heads=d_heads):
            grad = 0.0
            at = 0
            for part in normed:
                rows = part.shape[0]
                grad += dot(beside(d_heads, slice(at, at + rows)), part[...], 0, 0)
                at += rows
            grad = grad.T
            store(grad)
            sums(weight, grad, (beside(d_heads),))

    @pl.when(param == 3)
    def _():
        store(dot(beside(drel), sinus[...], 0, 0).T)


def grad_heads(order, here, parts, normed, sinus, dq_own, dq_far, dk, dv, drel, wq, wk, wv, chunk, extra):
    width, cols = wq.shape[0], wq.shape[1] // 2
    weight = pl.BlockSpec((width, cols), lambda i, ids: (0, ids[0]))
    arrays = [*normed, sinus, *dq_own, *dq_far, *dk, *dv, *drel]
    rows = width // chunk * (chunk + extra)
    return order.call(
        partial(grad_heads_kernel, parts, len(dk), chunk, extra),
        "grad_heads",
        [here],
        arrays + [wq, wk, wv],
        (4,),
        [whole(*a.shape) for a in arrays] + [weight] * 3,
        [pl.BlockSpec((rows, cols), lambda i, ids: (i, 0)), whole(width, 1), whole(width, 1)],
        [shape(4 * rows, cols)] + [shape(width, 1, wide)] * 2,
    )


def finish_kernel(ids, segment, d_hidden, own, received, gain, out):
    values = segment[...].astype(wide)
    centred = values - jnp.mean(values, -1, keepdims=True)
    inverse = lax.rsqrt(jnp.mean(centred * centred, -1, keepdims=True) + epsilon)
    normal = centred * inverse
    scaled = (own[...] + received[...].astype(wide)) * gain[...].astype(wide)
    inner = (
        scaled
        - jnp.mean(scaled, -1, keepdims=True)
        - normal * jnp.mean(scaled * normal, -1, keepdims=True)
    )
    out[...] = (d_hidden[...] + inner * inverse).astype(narrow)


def finish(order, *arrays):
    segment, d_hidden, own, received, gain = arrays
    arrays = [segment, d_hidden, own, received, gain[None]]
    return order.call(
        finish_kernel,
        "finish",
        [0],
        arrays,
        (1,),
        [whole(*a.shape) for a in arrays],
        whole(*segment.shape),
        shape(*segment.shape),
    )


def sinus_table():
    fine = 64
    frequency = 10000.0 ** (-2.0 * jnp.arange(D // 2, dtype=wide) / D)
    coarse_place = KEYS - 1 - fine * jnp.arange(KEYS // fine, dtype=wide)
    fine_place = jnp.arange(fine, dtype=wide)
    coarse = (coarse_place[:, None] * frequency[None, :])[:, None, :]
    little = (fine_place[:, None] * frequency[None, :])[None, :, :]
    sin_a, cos_a, sin_b, cos_b = lax.optimization_barrier(
        (jnp.sin(coarse), jnp.cos(coarse), jnp.sin(little), jnp.cos(little))
    )
    sine = sin_a * cos_b - cos_a * sin_b
    cosine = cos_a * cos_b + sin_a * sin_b
    return jnp.concatenate([sine, cosine], -1).astype(narrow).reshape(KEYS, D)


def matmul(left, right):
    return jnp.dot(left, right, preferred_element_type=wide)


def outer(left, right):
    return dot(left, right, 0, 0)


def on_device(
    segment,
    memory,
    comp_memory,
    mem_start,
    first_gain,
    first_bias,
    w_query,
    w_key,
    w_value,
    w_rel,
    u_bias,
    v_bias,
    w_out,
    second_gain,
    second_bias,
    w_up,
    b_up,
    w_down,
    b_down,
    w_comp,
    b_comp,
    cot_out,
    cot_comp,
):
    here, blocks = lax.axis_index("blk"), lax.axis_size("blk")
    segment, memory, comp_memory = segment[0], memory[0], comp_memory[0]
    cot_out, cot_comp = cot_out[0], cot_comp[0]
    rows, width = segment.shape
    heads = H // blocks
    cols = heads * DH
    parts = (comp_memory.shape[0], memory.shape[0], rows)
    block = sum(parts)
    count = lax.axis_size("dp").bit_length() - 1
    core, blk = ("dp", 0), ("blk", 0)
    near = [("dp", 1)]
    rest = [("dp", bit) for bit in range(2, count)]
    mate = side(*core)

    order = Order()
    weights = (first_gain, first_bias, w_query, w_key, w_value)

    windows = memory.reshape(parts[1] // RATE, RATE * width)
    far_seg = swap(segment, *blk)
    far_rest = swap(jnp.concatenate([memory, comp_memory], 0), *blk)
    cot_mate = swap(cot_out, *core)

    new_compressed = (matmul(windows, w_comp) + b_comp.astype(wide)).astype(narrow)
    grad_b_comp = jnp.sum(cot_comp.astype(wide), 0)
    grad_comp = outer(windows, cot_comp).astype(narrow)

    sinus = sinus_table()
    relative = matmul(sinus, lax.dynamic_slice_in_dim(w_rel, here * cols, cols, 1)).astype(narrow)

    own_seg, own_mem, own_comp, q_own = project(
        order, here, (segment, memory, comp_memory), (rows, parts[1], parts[0]), True, weights, cols
    )
    far_seg, q_far = project(
        order, here, [far_seg], (rows,), True, weights, cols, after=[relative, new_compressed, grad_comp]
    )
    far_mem, far_comp = project(
        order, here, [far_rest], (parts[1], parts[0]), False, weights, cols
    )
    own, other = (own_comp, own_mem, own_seg), (far_comp, far_mem, far_seg)
    comp_share = lax.psum_scatter(gate(order, grad_comp), ("dp", "blk"), scatter_dimension=0, tiled=True)
    inputs = [q_own, q_far, u_bias, v_bias]
    for part in (1, 2):
        inputs += [[t[part] for t in own], [t[part] for t in other]]
    inputs += [relative]
    mine, received, probs = [], [], []
    per = heads // 2
    for first in range(0, heads, per):
        own_heads, far_heads, kept = attend(order, here, mem_start[0], parts, inputs, first, per)
        mine.append(own_heads)
        received.append(swap(far_heads, *blk))
        probs.append(kept)

    (
        layer_out,
        packed,
        attended_keep,
        gelu_theirs,
        gelu_mine,
        d_pre_theirs,
        d_pre_mine,
        d_hidden,
        da_mine,
        da_theirs,
        grad_b_up,
        grad_second_gain,
        grad_second_bias,
        grad_b_down,
    ) = middle(
        order, here, mate, mine, received, segment, cot_out, w_out, second_gain, second_bias, w_up, b_up, w_down, b_down
    )

    gelu_mate = swap(gelu_theirs, *core)
    da_far = swap(da_theirs, *blk)
    d_pre_mate = swap(d_pre_theirs, *core)
    packed_mate = swap(packed, *core)
    units = gelu_mine.shape[1]
    jobs = (
        ("grad_down", near + [blk] + rest, (gelu_mine, 0, units), (gelu_mate, 0, units), (cot_out, 0, width), (cot_mate, 0, width)),
        ("grad_up", [blk] + near + rest, (packed, 0, width), (packed_mate, 0, width), (d_pre_mine, 0, units), (d_pre_mate, 0, units)),
        ("grad_out", rest + near + [blk], (attended_keep, 0, cols), (packed_mate, 2 * width, cols), (packed, width, width), (packed_mate, width, width)),
    )
    send = [
        outer_pair(order, *job[2:], 1 - side(*job[1][0]), job[0], after=[da_far] if job is jobs[1] else [])
        for job in jobs
    ]
    keep = [outer_pair(order, *job[2:], side(*job[1][0]), job[0]) for job in jobs]
    middle_steps = [job[1] for job in jobs]
    middle_sum = Scatter(order, "sum_middle", list(zip(send, keep, middle_steps)))

    back = []
    for number in range(2):
        back.append(attend_back(order, here, parts, probs[number], inputs, da_mine, da_far, number * per, per))
        middle_sum.step(4 if number == 0 else 2)
        if number == 0:
            comp_gathered = lax.all_gather(gate(order, comp_share), ("dp", "blk"), axis=0, tiled=True)
    dq_own, dq_far, d_key, d_value, d_relative, grad_u, grad_v = zip(*back)
    normed = [t[0] for t in own + other]
    chunk, extra = 4 * width // lax.axis_size("dp"), 16
    grads, by_gain, by_bias = grad_heads(
        order, here, parts, normed, sinus, dq_own, dq_far, d_key, d_value, d_relative, w_query, w_key, w_value, chunk, extra
    )
    middle_sum.step()
    grads, by_gain, by_bias = gate(order, grads, by_gain, by_bias)

    grad_first_bias = by_bias.reshape(width)
    grad_first_gain = (by_gain.reshape(width) - first_bias.astype(wide) * grad_first_bias) / first_gain.astype(wide)

    def spread(vectors):
        return lax.dynamic_update_slice_in_dim(
            jnp.zeros((width,), wide), jnp.concatenate(vectors, 1).reshape(cols), here * cols, 0
        )

    vectors = [
        grad_first_gain,
        grad_first_bias,
        spread(grad_u),
        spread(grad_v),
        grad_second_gain.reshape(-1),
        grad_second_bias.reshape(-1),
        grad_b_up.reshape(-1),
        grad_b_down.reshape(-1),
        grad_b_comp,
    ]

    shares = lax.axis_size("dp")
    beside = jnp.concatenate(vectors).reshape(-1, cols)
    upper = beside.astype(narrow)
    beside = jnp.concatenate([upper, (beside - upper.astype(wide)).astype(narrow)], 0)
    per = -(-beside.shape[0] // shares)
    beside = jnp.pad(beside, ((0, per * shares - beside.shape[0]), (0, 0))).reshape(shares, per, cols)
    grads = lax.dynamic_update_slice(grads.reshape(shares, chunk + extra, cols), beside, (0, chunk, 0))
    heads_share = lax.psum_scatter(grads, "dp", scatter_dimension=0, tiled=True)

    d_normed_own, d_normed_far = segment_back(
        order, here, dq_own, dq_far, d_key, d_value, w_query, w_key, w_value, block
    )
    middle_sum.step()
    d_normed_received = swap(gate(order, d_normed_far), *blk)
    middle_gather = Gather(
        order, "join_middle", [(share, steps[1:]) for share, steps in zip(middle_sum.keep, middle_steps)]
    )
    middle_gather.step()
    d_segment = finish(order, segment, d_hidden, d_normed_own, d_normed_received, first_gain)
    full_comp = widen(order, comp_gathered, "full_comp")
    middle_gather.step()
    heads_gathered = lax.all_gather(gate(order, heads_share), ("dp", "blk"), axis=0, tiled=True)
    middle_gather.step()
    down_pieces, up_pieces, out_pieces = (
        four_pieces(value, core, steps[0]) for value, steps in zip(middle_gather.values, middle_steps)
    )
    sums = heads_gathered[:, chunk : chunk + per].astype(wide).reshape(shares, blocks, per, cols)
    sums = jnp.sum(sums, 1).reshape(shares * per, cols)
    small = sum(vector.shape[0] for vector in vectors) // cols
    sums = (sums[:small] + sums[small : 2 * small]).reshape(-1)
    split = []
    at = 0
    for vector in vectors:
        split.append(sums[at : at + vector.shape[0]])
        at += vector.shape[0]

    devices = 2 << count

    def gathered(share, steps):
        return four_pieces(gather_rows(share, steps[1:]), core, steps[0])

    def by_rows(pieces, outer, inner, total_rows, name):
        blocks = 1 << len(inner)
        chunk = total_rows // len(pieces) // blocks
        (out,) = assemble(
            order,
            pieces,
            blocks,
            [place_of(outer), place_of(inner)],
            [(total_rows, width)],
            (total_rows // len(pieces), width // 2),
            lambda outer_place, part: (outer_place, part),
            lambda inner_place: (inner_place * chunk, 0),
            2,
            name,
        )
        return out

    full_out = by_rows(out_pieces, [core, middle_steps[2][0]], middle_steps[2][1:], width, "full_out")
    full_down = by_rows(down_pieces, [core, middle_steps[0][0]], middle_steps[0][1:], FF, "full_down")
    up_rows = width * 2 // devices
    (full_up,) = assemble(
        order,
        up_pieces,
        devices // 4,
        [place_of([core, middle_steps[1][0]]), place_of(middle_steps[1][1:])],
        [(width, FF)],
        (width // 2, FF // 4),
        lambda outer_place, part: (outer_place % 2, outer_place // 2 * 2 + part),
        lambda inner_place: (inner_place * up_rows, 0),
        2,
        "full_up",
    )
    full_query, full_key, full_value, full_rel = widen_heads(
        order, heads_gathered.reshape(-1, cols), chunk, extra, width, cols, "full_heads"
    )

    return (
        layer_out[None],
        d_segment[None],
        new_compressed[None],
        split[0],
        split[1],
        full_query,
        full_key,
        full_value,
        full_rel,
        split[2],
        split[3],
        full_out,
        split[4],
        split[5],
        full_up,
        split[6],
        full_down,
        split[7],
        full_comp,
        split[8],
    )


def solution(mesh):
    rows = P("dp", "blk", None)
    in_specs = (rows,) * 3 + (P("dp"),) + (P(),) * 17 + (rows,) * 2
    out_specs = (rows,) * 3 + (P(),) * 17
    return jax.shard_map(
        on_device, mesh=mesh, in_specs=in_specs, out_specs=out_specs, check_vma=False
    )
```

```python
from functools import partial

import jax
import jax.numpy as jnp
from jax import lax
from jax.experimental import pallas as pl
from jax.experimental.pallas import tpu as pltpu
from jax.sharding import PartitionSpec as P

D = 1024
H = 8
DH = 128
FF = 4096
CMEM = 512
RATE = 3
KEYS = 2432

TILE = 192
FF_TILE = 512
epsilon = 1e-05
negative = -1e30
wide = jnp.float32
narrow = jnp.bfloat16
MIB = 1 << 20


def dot(left, right, left_dim, right_dim):
    return lax.dot_general(
        left, right, (((left_dim,), (right_dim,)), ((), ())), preferred_element_type=wide
    )


def shape(rows, cols, dtype=narrow):
    return jax.ShapeDtypeStruct((rows, cols), dtype)


def whole(rows, cols):
    return pl.BlockSpec((rows, cols), lambda *_: (0, 0))


class Order:
    def __init__(self):
        self.last = []

    def call(self, kernel, name, scalars, arrays, grid, in_specs, out_specs, out_shape, scratch=(), after=(), aliases=()):
        count = len(arrays)
        after = list(after) + self.last

        def body(scalar_ref, *refs):
            kernel(scalar_ref, *refs[:count], *refs[count + len(after) :])

        out = pl.pallas_call(
            body,
            grid_spec=pltpu.PrefetchScalarGridSpec(
                num_scalar_prefetch=1,
                grid=grid,
                in_specs=list(in_specs) + [pl.BlockSpec(memory_space=pl.ANY)] * len(after),
                out_specs=out_specs,
                scratch_shapes=list(scratch),
            ),
            out_shape=out_shape,
            input_output_aliases={1 + i: o for i, o in aliases},
            compiler_params=pltpu.CompilerParams(vmem_limit_bytes=60 * MIB),
            cost_estimate=pl.CostEstimate(
                flops=1000, bytes_accessed=1000, transcendentals=0
            ),
            name=name,
        )(jnp.stack([jnp.asarray(s, jnp.int32) for s in scalars]), *arrays, *after)
        self.last = [out[-1] if isinstance(out, (list, tuple)) else out]
        return out


def swap(value, axis, bit=0):
    pairs = [(source, source ^ (1 << bit)) for source in range(lax.axis_size(axis))]
    return lax.ppermute(value, axis, pairs)


def side(axis, bit=0):
    return (lax.axis_index(axis) >> bit) & 1


def place_of(steps):
    place = jnp.int32(0)
    for axis, bit in steps:
        place = place * 2 + side(axis, bit)
    return place


def add_split(order, chains, steps, name):
    in_specs, out_specs, out_shape, arrays = [], [], [], []
    for number, (kept, received, _) in enumerate(chains):
        rows, cols = kept.shape
        block = rows // 2 // steps
        theirs = pl.BlockSpec((block, cols), lambda i, ids, n=number: ((1 - ids[n]) * steps + i, 0))
        ours = pl.BlockSpec((block, cols), lambda i, ids, n=number: (ids[n] * steps + i, 0))
        arrays += [kept, received, kept, received]
        in_specs += [theirs, theirs, ours, ours]
        out_specs += [pl.BlockSpec((block, cols), lambda i, ids: (i, 0))] * 2
        out_shape += [shape(rows // 2, cols)] * 2

    def kernel(ids, *refs):
        ins, outs = refs[: 4 * len(chains)], refs[4 * len(chains) :]
        for number, out in enumerate(outs):
            a, b = ins[2 * number], ins[2 * number + 1]
            out[...] = (a[...].astype(wide) + b[...].astype(wide)).astype(narrow)

    out = order.call(kernel, name, [c[2] for c in chains], arrays, (steps,), in_specs, out_specs, out_shape)
    return [(out[2 * n], out[2 * n + 1]) for n in range(len(chains))]


def add(order, pairs, name):
    arrays = [value for pair in pairs for value in pair]

    def kernel(ids, *refs):
        for number, out in enumerate(refs[len(arrays) :]):
            a, b = refs[2 * number], refs[2 * number + 1]
            out[...] = (a[...].astype(wide) + b[...].astype(wide)).astype(narrow)

    return order.call(
        kernel,
        name,
        [0],
        arrays,
        (1,),
        [whole(*a.shape) for a in arrays],
        [whole(*a.shape) for a, _ in pairs],
        [shape(*a.shape) for a, _ in pairs],
    )


def gate(order, *values):
    place = pl.BlockSpec(memory_space=pl.ANY)
    out = order.call(
        lambda ids, *refs: None,
        "gate",
        [0],
        values,
        (1,),
        [place] * len(values),
        [place] * len(values),
        [jax.ShapeDtypeStruct(value.shape, value.dtype) for value in values],
        aliases=[(n, n) for n in range(len(values))],
    )
    return out[0] if len(values) == 1 else out


class Scatter:
    def __init__(self, order, name, chains):
        self.order, self.name = order, name
        self.steps = [steps for _, _, steps in chains]
        self.keep = [keep for _, keep, _ in chains]
        self.received = [swap(send, *steps[0]) for send, _, steps in chains]
        self.at = 0

    def step(self, blocks=1):
        self.at += 1
        if self.at == len(self.steps[0]):
            self.keep = add(self.order, list(zip(self.keep, self.received)), self.name)
            return self.keep
        chains = [
            (keep, received, side(*steps[self.at]))
            for keep, received, steps in zip(self.keep, self.received, self.steps)
        ]
        halves = add_split(self.order, chains, blocks, self.name)
        self.keep = [keep for _, keep in halves]
        self.received = [swap(send, *steps[self.at]) for (send, _), steps in zip(halves, self.steps)]


def join(order, pairs, name):
    arrays = [value for pair in pairs for value in pair]

    def kernel(ids, *refs):
        for number, out in enumerate(refs[len(arrays) :]):
            a, b = refs[2 * number], refs[2 * number + 1]
            rows = a.shape[0]
            out[0:rows, :] = a[...]
            out[rows:, :] = b[...]

    outs = [(2 * a.shape[0], a.shape[1]) for a, _ in pairs]
    return order.call(
        kernel,
        name,
        [0],
        arrays,
        (1,),
        [whole(*a.shape) for a in arrays],
        [whole(*out) for out in outs],
        [shape(*out) for out in outs],
    )


class Gather:
    def __init__(self, order, name, chains):
        self.order, self.name = order, name
        self.values = [value for value, _ in chains]
        self.steps = [list(steps) for _, steps in chains]
        self.send()

    def send(self):
        self.received = [swap(value, *steps.pop()) for value, steps in zip(self.values, self.steps)]

    def step(self):
        self.values = join(self.order, list(zip(self.values, self.received)), self.name)
        if self.steps[0]:
            self.send()


def assemble(order, pieces, whose, blocks, places, out_shape, out_block, index, inside, splits, name, before=None):
    rows, cols = pieces[0].shape
    chunk, part = rows // blocks, cols // splits
    count = len(pieces)

    def kernel(ids, *refs):
        out = refs[-1]
        number = pl.program_id(0)

        def copy(ref):
            for r in range(blocks):
                row, col = inside(r ^ ids[1])
                out[pl.ds(pl.multiple_of(row, 8), chunk), pl.ds(pl.multiple_of(col, 128), part)] = ref[
                    r * chunk : (r + 1) * chunk, :
                ].astype(wide)

        for n, ref in enumerate(refs[:count]):
            pl.when(number == n)(partial(copy, ref))

    def piece_spec(n):
        return pl.BlockSpec(
            (rows, part), lambda i, j, ids: (0, jnp.where(i == n, j, jnp.where(i < n, 0, splits - 1)))
        )

    def out_index(i, j, ids):
        outer_place = whose[0]
        for n, place in enumerate(whose[1:]):
            outer_place = jnp.where(i == n + 1, place, outer_place)
        return index(outer_place ^ ids[0], j)

    more = [] if before is None else [before]
    return order.call(
        kernel,
        name,
        places,
        list(pieces) + more,
        (count, splits),
        [piece_spec(n) for n in range(count)] + [pl.BlockSpec(memory_space=pl.ANY)] * len(more),
        pl.BlockSpec(out_block, out_index),
        shape(*out_shape, wide),
        aliases=[(count, 0)] if more else [],
    )


def widen(order, value, name):
    rows, cols = value.shape
    steps = 4

    def kernel(ids, ref, out):
        out[...] = ref[...].astype(wide)

    at = pl.BlockSpec((rows // steps, cols), lambda i, ids: (i, 0))
    return order.call(kernel, name, [0], [value], (steps,), [at], at, shape(rows, cols, wide))


def widen_heads(order, gathered, chunk, extra, width, cols, name, after):
    arrays = 4
    rows = gathered.shape[0] // arrays
    count = rows // (chunk + extra)

    def kernel(ids, ref, *outs):
        def copy(out):
            for r in range(count):
                at = r * (chunk + extra)
                row, col = r // 2 * chunk, r % 2 * cols
                out[row : row + chunk, col : col + cols] = ref[at : at + chunk, :].astype(wide)

        for number, out in enumerate(outs):
            pl.when(pl.program_id(0) == number)(partial(copy, out))

    return order.call(
        kernel,
        name,
        [0],
        [gathered],
        (arrays,),
        [pl.BlockSpec((rows, cols), lambda i, ids: (i, 0))],
        [whole(width, width)] * arrays,
        [shape(width, width, wide)] * arrays,
        after=after,
    )


def project_kernel(count, lengths, ids, *refs):
    parts, (gain, bias, wq, wk, wv), outs = refs[:count], refs[count : count + 5], refs[count + 5 :]
    if count < len(lengths):
        firsts = [sum(lengths[:n]) for n in range(len(lengths))]
        parts = [parts[0].at[first : first + length, :] for first, length in zip(firsts, lengths)]
        count = len(lengths)
    for number, part in enumerate(parts):
        normed, k, v = outs[3 * number : 3 * number + 3]
        values = part[...].astype(wide)
        centred = values - jnp.mean(values, -1, keepdims=True)
        inverse = lax.rsqrt(jnp.mean(centred * centred, -1, keepdims=True) + epsilon)
        low = (centred * inverse * gain[...].astype(wide) + bias[...].astype(wide)).astype(narrow)
        normed[...] = low
        k[...] = dot(low, wk[...], 1, 0).astype(narrow)
        v[...] = dot(low, wv[...], 1, 0).astype(narrow)
        if number == 0 and len(outs) > 3 * count:
            outs[-1][...] = dot(low, wq[...], 1, 0)


def project(order, here, parts, lengths, query, weights, cols, after=()):
    gain, bias, wq, wk, wv = weights
    width = wq.shape[0]
    weight = pl.BlockSpec((width, cols), lambda i, ids: (0, ids[0]))
    unused = whole(16, 128)
    out_shape = [s for n in lengths for s in (shape(n, width), shape(n, cols), shape(n, cols))]
    if query:
        out_shape.append(shape(lengths[0], cols, wide))
    out = order.call(
        partial(project_kernel, len(parts), lengths),
        "project",
        [here],
        list(parts) + [gain[None], bias[None], wq, wk, wv],
        (1,),
        [whole(*p.shape) for p in parts] + [whole(1, width)] * 2 + [weight if query else unused, weight, weight],
        [whole(*o.shape) for o in out_shape],
        out_shape,
        after=after,
    )
    triples = [tuple(out[3 * n : 3 * n + 3]) for n in range(len(lengths))]
    return triples + ([out[-1]] if query else [])


def tiles_of(seg, keys, tile):
    tiles = []
    for first in range(0, seg, tile):
        used = keys - seg + first + tile
        cols = -(-used // 128) * 128
        tiles.append((first, cols, keys - cols, cols - used))
    return tiles


def turned(values):
    order = 7 - lax.broadcasted_iota(jnp.int32, (8, values.shape[1]), 0)
    parts = [jnp.take_along_axis(values[at : at + 8], order, 0) for at in range(0, values.shape[0], 8)]
    return jnp.concatenate(parts, 0)


def unskew(grid, tile, cols, pad):
    parts = []
    order = 7 - lax.broadcasted_iota(jnp.int32, (8, cols), 0)
    for at in range(0, tile, 8):
        rows = jnp.take_along_axis(grid[at : at + 8], order, 0)
        parts.append(pltpu.roll(rows, tile - 1 + pad - at - 7, 1, stride=1, stride_axis=0))
    return jnp.concatenate(parts, 0)


def spans(parts, here):
    out = []
    at = 0
    for length in parts:
        own = pl.multiple_of(2 * at + here * length, 16)
        far = pl.multiple_of(2 * at + (1 - here) * length, 16)
        out.append((pl.ds(at, length), pl.ds(own, length), pl.ds(far, length)))
        at += length
    return out


def place_parts(parts, here, own, far, out):
    for (_, own_rows, far_rows), own_part, far_part in zip(spans(parts, here), own, far):
        out[own_rows, :] = own_part[...]
        out[far_rows, :] = far_part[...]


def place_queries(parts, here, q_own, q_far, u, v, qc, qp):
    ((_, own_rows, far_rows),) = spans(parts[2:], here)
    for ref, rows in ((q_own, own_rows), (q_far, far_rows)):
        qc[rows, :] = (ref[...] + u[...].astype(wide)).astype(narrow)
        qp[rows, :] = (ref[...] + v[...].astype(wide)).astype(narrow)


def attend_kernel(parts, ids, q_own, q_far, u, v, *refs):
    k_own, k_far, v_own, v_far = refs[0:3], refs[3:6], refs[6:9], refs[9:12]
    rel, out_own, out_far, probs_ref, qc, qp, ks, vs, outs = refs[12:]
    here, start = ids[0], ids[1]
    place_queries(parts, here, q_own, q_far, u, v, qc, qp)
    place_parts(parts, here, k_own, k_far, ks)
    place_parts(parts, here, v_own, v_far, vs)
    seg, keys = qc.shape[0], ks.shape[0]
    past = keys - seg
    factor = DH**-0.5 * 1.4426950408889634
    for first, cols, base, pad in tiles_of(seg, keys, TILE):
        rows = pl.ds(first, TILE)
        content = dot(qc[rows, :], ks[0:cols, :], 1, 1)
        table = dot(qp[rows, :], rel[base : base + cols, :], 1, 1)
        table = pltpu.roll(table, cols - (TILE - 1 + pad), 1, stride=1, stride_axis=0)
        scores = content + table
        left = scores[:, :CMEM]
        lane = lax.broadcasted_iota(jnp.int32, left.shape, 1)
        left = jnp.where(lane >= start, left, negative)
        edge = (past + first) // 128 * 128
        right = scores[:, edge:]
        lane = lax.broadcasted_iota(jnp.int32, right.shape, 1) + (edge - past - first)
        row = lax.broadcasted_iota(jnp.int32, right.shape, 0)
        right = jnp.where(lane <= row, right, negative)
        scores = jnp.concatenate([left, scores[:, CMEM:edge], right], 1)
        largest = jnp.max(scores, -1, keepdims=True)
        probs = jnp.exp2(scores * factor - largest * factor)
        probs = (probs * (1.0 / jnp.sum(probs, -1, keepdims=True))).astype(narrow)
        probs_ref[0, rows, 0:cols] = probs
        outs[rows, :] = dot(probs, vs[0:cols, :], 1, 0).astype(narrow)
    ((_, own_rows, far_rows),) = spans(parts[2:], here)
    out_own[...] = outs[own_rows, :]
    out_far[...] = outs[far_rows, :]


def part_specs(parts, first):
    return [pl.BlockSpec((length, DH), lambda h, ids: (0, h + first)) for length in parts]


def attend(order, here, start, parts, inputs, first, heads):
    q_own, q_far, u, v, k_own, k_far, v_own, v_far, rel = inputs
    rows, keys = parts[2], rel.shape[0]
    query = pl.BlockSpec((rows, DH), lambda h, ids: (0, h + first))
    bias = pl.BlockSpec((1, DH), lambda h, ids: (0, h + first + ids[0] * (H // 2)))
    out = pl.BlockSpec((rows, DH), lambda h, ids: (0, h))
    seg = 2 * rows
    return order.call(
        partial(attend_kernel, parts),
        "attend",
        [here, start],
        [q_own, q_far, u[None], v[None], *k_own, *k_far, *v_own, *v_far, rel],
        (heads,),
        [query, query, bias, bias]
        + part_specs(parts, first) * 4
        + [pl.BlockSpec((keys, DH), lambda h, ids: (0, h + first))],
        [out, out, pl.BlockSpec((1, seg, keys), lambda h, ids: (h, 0, 0))],
        [shape(rows, heads * DH)] * 2 + [jax.ShapeDtypeStruct((heads, seg, keys), narrow)],
        [pltpu.VMEM((seg, DH), narrow)] * 2
        + [pltpu.VMEM((keys, DH), narrow)] * 2
        + [pltpu.VMEM((seg, DH), narrow)],
    )


def attend_back_kernel(parts, ids, probs_ref, q_own, q_far, u, v, *refs):
    k_own, k_far, v_own, v_far = refs[0:3], refs[3:6], refs[6:9], refs[9:12]
    rel, da_own, da_far, dq_own, dq_far, dk_ref, dv_ref, drel_ref, gu_ref, gv_ref = refs[12:22]
    qc_ref, qp_ref, ks, vs, das, dqs, stage, key_sum, value_sum, rel_sum = refs[22:]
    here = ids[0]
    place_queries(parts, here, q_own, q_far, u, v, qc_ref, qp_ref)
    place_parts(parts, here, k_own, k_far, ks)
    place_parts(parts, here, v_own, v_far, vs)
    ((_, own_rows, far_rows),) = spans(parts[2:], here)
    das[own_rows, :] = da_own[...]
    das[far_rows, :] = da_far[...]
    seg, keys = qc_ref.shape[0], ks.shape[0]
    scale = DH**-0.5

    grad_u = jnp.zeros((1, DH), wide)
    grad_v = jnp.zeros((1, DH), wide)
    for step, (first, cols, base, pad) in enumerate(tiles_of(seg, keys, TILE)[::-1]):
        rows = pl.ds(first, TILE)
        probs = probs_ref[0, rows, 0:cols]
        probs_wide = probs.astype(wide)
        d_out, qc, qp = das[rows, :], qc_ref[rows, :], qp_ref[rows, :]
        d_probs = dot(d_out, vs[0:cols, :], 1, 1)
        weighted = probs_wide * d_probs
        d_scores = weighted - probs_wide * jnp.sum(weighted, -1, keepdims=True)
        d_low = d_scores.astype(narrow)
        d_table = unskew(d_scores, TILE, cols, pad).astype(narrow)
        d_content = dot(d_low, ks[0:cols, :], 1, 0)
        d_position = turned(dot(d_table, rel[base : base + cols, :], 1, 0))
        grad_u += jnp.sum(d_content, 0, keepdims=True)
        grad_v += jnp.sum(d_position, 0, keepdims=True)
        dqs[rows, :] = ((d_content + d_position) * scale).astype(narrow)
        d_key = dot(qc, d_low, 0, 0)
        d_value = dot(d_out, probs, 0, 0)
        d_rel = dot(turned(qp.astype(wide)).astype(narrow), d_table, 0, 0)
        if step == 0:
            key_sum[...] = d_key
            value_sum[...] = d_value
            rel_sum[...] = d_rel
        else:
            key_sum[:, 0:cols] += d_key
            value_sum[:, 0:cols] += d_value
            rel_sum[:, base : base + cols] += d_rel
    gu_ref[...] = grad_u * scale
    gv_ref[...] = grad_v * scale
    drel_ref[...] = (rel_sum[...] * scale).T.astype(narrow)
    dq_own[...] = dqs[own_rows, :]
    dq_far[...] = dqs[far_rows, :]
    block = sum(parts)
    for total, factor, out in ((key_sum, scale, dk_ref), (value_sum, 1.0, dv_ref)):
        stage[...] = (total[...] * factor).T.astype(narrow)
        for rows, mine, theirs in spans(parts, here):
            out[rows, :] = stage[mine, :]
            out[pl.ds(block + rows.start, rows.size), :] = stage[theirs, :]


def attend_back(order, here, parts, probs, inputs, da_own, da_far, first, heads):
    q_own, q_far, u, v, k_own, k_far, v_own, v_far, rel = inputs
    rows, keys = parts[2], rel.shape[0]
    seg = 2 * rows
    query = pl.BlockSpec((rows, DH), lambda h, ids: (0, h + first))
    bias = pl.BlockSpec((1, DH), lambda h, ids: (0, h + first + ids[0] * (H // 2)))
    key = pl.BlockSpec((keys, DH), lambda h, ids: (0, h + first))
    query_out = pl.BlockSpec((rows, DH), lambda h, ids: (0, h))
    key_out = pl.BlockSpec((keys, DH), lambda h, ids: (0, h))
    per_head = pl.BlockSpec((1, DH), lambda h, ids: (0, h))
    small, large = pltpu.VMEM((seg, DH), narrow), pltpu.VMEM((keys, DH), narrow)
    return order.call(
        partial(attend_back_kernel, parts),
        "attend_back",
        [here],
        [probs, q_own, q_far, u[None], v[None], *k_own, *k_far, *v_own, *v_far, rel, da_own, da_far],
        (heads,),
        [pl.BlockSpec((1, seg, keys), lambda h, ids: (h, 0, 0)), query, query, bias, bias]
        + part_specs(parts, first) * 4
        + [key, query, query],
        [query_out, query_out, key_out, key_out, key_out, per_head, per_head],
        [shape(rows, heads * DH)] * 2
        + [shape(keys, heads * DH)] * 3
        + [shape(1, heads * DH, wide)] * 2,
        [small, small, large, large, small, small, large] + [pltpu.VMEM((DH, keys), wide)] * 3,
    )


def middle_kernel(own_pieces, far_pieces, ids, *refs):
    mine, refs = refs[:own_pieces], refs[own_pieces:]
    received, refs = refs[:far_pieces], refs[far_pieces:]
    segment, cot, w_out, gain, bias, w_up, b_up, w_down, b_down = refs[:9]
    (layer_out, packed, att_keep, gelu_theirs, gelu_mine, d_theirs, d_mine, d_hidden, da_mine, da_theirs, g_up, g_gain, g_bias, g_down,
     normal, inverse, layer, back) = refs[9:]
    normed, d_branch, att_send = packed.at[:, 0:D], packed.at[:, D : 2 * D], packed.at[:, 2 * D :]
    step = pl.program_id(0)
    steps = pl.num_programs(0)
    here = ids[0]
    half = D // 2

    @pl.when(step == 0)
    def _():
        own = jnp.concatenate([ref[...] for ref in mine], 1)
        far = jnp.concatenate([ref[...] for ref in received], 1)
        own_rows = pl.ds(pl.multiple_of(here * half, 128), half)
        far_rows = pl.ds(pl.multiple_of((1 - here) * half, 128), half)
        hidden = segment[...].astype(wide) + dot(own, w_out[own_rows, :], 1, 0) + dot(far, w_out[far_rows, :], 1, 0)
        same = here == ids[1]
        att_keep[...] = jnp.where(same, own, far)
        att_send[...] = jnp.where(same, far, own)
        centred = hidden - jnp.mean(hidden, -1, keepdims=True)
        scale = lax.rsqrt(jnp.mean(centred * centred, -1, keepdims=True) + epsilon)
        inverse[...] = scale
        normal[...] = centred * scale
        normed[...] = (normal[...] * gain[...].astype(wide) + bias[...].astype(wide)).astype(narrow)
        layer[...] = hidden + b_down[...].astype(wide)
        back[...] = jnp.zeros_like(back)

    t = dot(normed[...], w_up[...], 1, 0) + b_up[...].astype(wide)
    d_gelu = dot(cot[...], w_down[...], 1, 1)
    square = t * t
    slope = 0.7978845608028654
    bent = jnp.tanh(slope * t * (1.0 + 0.044715 * square))
    rise = 0.5 * (1.0 + bent)
    gelu = (t * rise).astype(narrow)
    change = rise + (0.5 * slope) * t * (1.0 - bent * bent) * (1.0 + (3 * 0.044715) * square)
    d_pre = (d_gelu * change).astype(narrow)
    layer[...] += dot(gelu, w_down[...], 1, 0)
    back[...] += dot(d_pre, w_up[...], 1, 1)
    g_up[...] = jnp.sum(d_pre.astype(wide), 0, keepdims=True)

    @pl.when(step < steps // 2)
    def _():
        gelu_theirs[...] = gelu
        d_theirs[...] = d_pre

    @pl.when(step >= steps // 2)
    def _():
        gelu_mine[...] = gelu
        d_mine[...] = d_pre

    @pl.when(step == steps - 1)
    def _():
        layer_out[...] = layer[...].astype(narrow)
        e, n = back[...], normal[...]
        cot_wide = cot[...].astype(wide)
        en = e * n
        g_gain[...] = jnp.sum(en, 0, keepdims=True)
        g_bias[...] = jnp.sum(e, 0, keepdims=True)
        g_down[...] = jnp.sum(cot_wide, 0, keepdims=True)
        by = gain[...].astype(wide)
        inner = e * by - jnp.mean(e * by, -1, keepdims=True) - n * jnp.mean(en * by, -1, keepdims=True)
        d_wide = cot_wide + inner * inverse[...]
        d_hidden[...] = d_wide
        low = d_wide.astype(narrow)
        d_branch[...] = low
        own_rows = pl.ds(pl.multiple_of(here * half, 128), half)
        far_rows = pl.ds(pl.multiple_of((1 - here) * half, 128), half)
        da_theirs[...] = dot(low, w_out[far_rows, :], 1, 1).astype(narrow)
        da_mine[...] = dot(low, w_out[own_rows, :], 1, 1).astype(narrow)


def middle(order, here, core, mine, received, segment, cot, w_out, gain, bias, w_up, b_up, w_down, b_down):
    rows, width = segment.shape
    units = w_up.shape[1]
    steps = units // FF_TILE
    half = steps // 2

    def tile(j, ids):
        return jnp.where(j < half, (1 - ids[1]) * half + j, ids[1] * half + j - half)

    up = pl.BlockSpec((width, FF_TILE), lambda j, ids: (0, tile(j, ids)))
    down = pl.BlockSpec((FF_TILE, width), lambda j, ids: (tile(j, ids), 0))
    unit = pl.BlockSpec((1, FF_TILE), lambda j, ids: (0, tile(j, ids)))
    theirs = pl.BlockSpec((rows, FF_TILE), lambda j, ids: (0, jnp.minimum(j, half - 1)))
    ours = pl.BlockSpec((rows, FF_TILE), lambda j, ids: (0, jnp.maximum(j - half, 0)))
    row, vector = whole(rows, width), whole(1, width)
    heads = whole(rows, width // 2)
    return order.call(
        partial(middle_kernel, len(mine), len(received)),
        "middle",
        [here, core],
        list(mine) + list(received) + [segment, cot, w_out, gain[None], bias[None], w_up, b_up[None], w_down, b_down[None]],
        (steps,),
        [whole(*a.shape) for a in list(mine) + list(received)]
        + [row, row, whole(width, width), vector, vector, up, unit, down, vector],
        [row, whole(rows, 5 * width // 2), heads, theirs, ours, theirs, ours, row, heads, heads, unit]
        + [vector] * 3,
        [shape(rows, width), shape(rows, 5 * width // 2), shape(rows, width // 2)]
        + [shape(rows, units // 2)] * 4
        + [shape(rows, width, wide)]
        + [shape(rows, width // 2)] * 2
        + [shape(1, units, wide)]
        + [shape(1, width, wide)] * 3,
        [pltpu.VMEM((rows, width), wide), pltpu.VMEM((rows, 1), wide)] + [pltpu.VMEM((rows, width), wide)] * 2,
    )


def outer_pairs(order, jobs, whichs, name, after=()):
    arrays, in_specs, out_specs, out_shape, spans_of = [], [], [], [], []
    step = 0
    for number, job in enumerate(jobs):
        rows, cols = job[0][2] // 2, job[2][2]
        block = min(rows, 512)
        first, steps = step, rows // block
        step += steps
        spans_of.append((first, steps))

        def at(i, first=first, steps=steps):
            return jnp.clip(i - first, 0, steps - 1)

        for array, column, _ in job[:2]:
            arrays.append(array)
            in_specs.append(
                pl.BlockSpec(
                    (array.shape[0], block),
                    lambda i, ids, n=number, c=column // block, steps=steps, at=at: (0, c + ids[n] * steps + at(i)),
                )
            )
        for array, column, _ in job[2:]:
            arrays.append(array)
            in_specs.append(pl.BlockSpec((array.shape[0], cols), lambda i, ids, c=column // cols: (0, c)))
        out_specs.append(pl.BlockSpec((block, cols), lambda i, ids, at=at: (at(i), 0)))
        out_shape.append(shape(rows, cols))

    def kernel(ids, *refs):
        number = pl.program_id(0)
        for n, (first, steps) in enumerate(spans_of):

            def run(n=n):
                lo, lf, ro, rf = refs[4 * n : 4 * n + 4]
                total = dot(lo[...], ro[...], 0, 0) + dot(lf[...], rf[...], 0, 0)
                refs[4 * len(jobs) + n][...] = total.astype(narrow)

            if len(jobs) == 1:
                run()
            else:
                pl.when((number >= first) & (number < first + steps))(run)

    return order.call(
        kernel, name, whichs, arrays, (step,), in_specs, out_specs, out_shape, after=after
    )


def segment_back_kernel(count, block, ids, *refs):
    dq_own, dq_far, dk, dv = (refs[n * count : (n + 1) * count] for n in range(4))
    wq, wk, wv, own, far = refs[4 * count :]
    rows = dq_own[0].shape[0]

    def through(dq, last):
        at = pl.ds(last - rows, rows)
        total = dot(jnp.concatenate([d[...] for d in dq], 1), wq[...], 1, 1)
        total += dot(jnp.concatenate([d[at, :] for d in dk], 1), wk[...], 1, 1)
        return total + dot(jnp.concatenate([d[at, :] for d in dv], 1), wv[...], 1, 1)

    far[...] = through(dq_far, 2 * block).astype(narrow)
    own[...] = through(dq_own, block)


def segment_back(order, here, dq_own, dq_far, dk, dv, wq, wk, wv, block):
    rows, width, cols = dq_own[0].shape[0], wq.shape[0], wq.shape[1] // 2
    weight = pl.BlockSpec((width, cols), lambda i, ids: (0, ids[0]))
    arrays = [*dq_own, *dq_far, *dk, *dv]
    return order.call(
        partial(segment_back_kernel, len(dk), block),
        "segment_back",
        [here],
        arrays + [wq, wk, wv],
        (1,),
        [whole(*a.shape) for a in arrays] + [weight] * 3,
        [whole(rows, width)] * 2,
        [shape(rows, width, wide), shape(rows, width)],
    )


def grad_heads_kernel(parts, count, chunk, extra, ids, *refs):
    normed, refs = refs[:6], refs[6:]
    sinus, refs = refs[0], refs[1:]
    dq_own, dq_far, dk, dv, drel = (refs[n * count : (n + 1) * count] for n in range(5))
    wq, wk, wv, out, by_gain, by_bias = refs[5 * count :]
    param = pl.program_id(0)

    @pl.when(param == 0)
    def _():
        by_gain[...] = jnp.zeros_like(by_gain)
        by_bias[...] = jnp.zeros_like(by_bias)

    def store(grad):
        for n in range(grad.shape[0] // chunk):
            at = n * (chunk + extra)
            out[at : at + chunk, :] = grad[n * chunk : (n + 1) * chunk, :].astype(narrow)
            out[at + chunk : at + chunk + extra, :] = jnp.zeros((extra, grad.shape[1]), narrow)

    def sums(weight, grad, d_heads):
        weight = weight[...].astype(wide)
        column = sum(jnp.sum(d.astype(wide), 0, keepdims=True) for d in d_heads)
        by_gain[...] += jnp.sum(weight * grad, 1, keepdims=True)
        by_bias[...] += jnp.sum(weight * column, 1, keepdims=True)

    def beside(refs, rows=slice(None)):
        return jnp.concatenate([ref[rows, :] for ref in refs], 1)

    @pl.when(param == 0)
    def _():
        own, far = beside(dq_own), beside(dq_far)
        grad = (dot(own, normed[2][...], 0, 0) + dot(far, normed[5][...], 0, 0)).T
        store(grad)
        sums(wq, grad, (own, far))

    for number, weight, d_heads in ((1, wk, dk), (2, wv, dv)):

        @pl.when(param == number)
        def _(weight=weight, d_heads=d_heads):
            grad = 0.0
            at = 0
            for part in normed:
                rows = part.shape[0]
                grad += dot(beside(d_heads, slice(at, at + rows)), part[...], 0, 0)
                at += rows
            grad = grad.T
            store(grad)
            sums(weight, grad, (beside(d_heads),))

    @pl.when(param == 3)
    def _():
        store(dot(beside(drel), sinus[...], 0, 0).T)


def grad_heads(order, here, parts, normed, sinus, dq_own, dq_far, dk, dv, drel, wq, wk, wv, chunk, extra):
    width, cols = wq.shape[0], wq.shape[1] // 2
    weight = pl.BlockSpec((width, cols), lambda i, ids: (0, ids[0]))
    arrays = [*normed, sinus, *dq_own, *dq_far, *dk, *dv, *drel]
    rows = width // chunk * (chunk + extra)
    return order.call(
        partial(grad_heads_kernel, parts, len(dk), chunk, extra),
        "grad_heads",
        [here],
        arrays + [wq, wk, wv],
        (4,),
        [whole(*a.shape) for a in arrays] + [weight] * 3,
        [pl.BlockSpec((rows, cols), lambda i, ids: (i, 0)), whole(width, 1), whole(width, 1)],
        [shape(4 * rows, cols)] + [shape(width, 1, wide)] * 2,
    )


def finish_kernel(ids, segment, d_hidden, own, received, gain, out):
    values = segment[...].astype(wide)
    centred = values - jnp.mean(values, -1, keepdims=True)
    inverse = lax.rsqrt(jnp.mean(centred * centred, -1, keepdims=True) + epsilon)
    normal = centred * inverse
    scaled = (own[...] + received[...].astype(wide)) * gain[...].astype(wide)
    inner = (
        scaled
        - jnp.mean(scaled, -1, keepdims=True)
        - normal * jnp.mean(scaled * normal, -1, keepdims=True)
    )
    out[...] = (d_hidden[...] + inner * inverse).astype(narrow)


def finish(order, *arrays):
    segment, d_hidden, own, received, gain = arrays
    arrays = [segment, d_hidden, own, received, gain[None]]
    return order.call(
        finish_kernel,
        "finish",
        [0],
        arrays,
        (1,),
        [whole(*a.shape) for a in arrays],
        whole(*segment.shape),
        shape(*segment.shape),
    )


def sinus_table():
    fine = 64
    frequency = 10000.0 ** (-2.0 * jnp.arange(D // 2, dtype=wide) / D)
    coarse_place = KEYS - 1 - fine * jnp.arange(KEYS // fine, dtype=wide)
    fine_place = jnp.arange(fine, dtype=wide)
    coarse = (coarse_place[:, None] * frequency[None, :])[:, None, :]
    little = (fine_place[:, None] * frequency[None, :])[None, :, :]
    sin_a, cos_a, sin_b, cos_b = lax.optimization_barrier(
        (jnp.sin(coarse), jnp.cos(coarse), jnp.sin(little), jnp.cos(little))
    )
    sine = sin_a * cos_b - cos_a * sin_b
    cosine = cos_a * cos_b + sin_a * sin_b
    return jnp.concatenate([sine, cosine], -1).astype(narrow).reshape(KEYS, D)


def matmul(left, right):
    return jnp.dot(left, right, preferred_element_type=wide)


def outer(left, right):
    return dot(left, right, 0, 0)


def on_device(
    segment,
    memory,
    comp_memory,
    mem_start,
    first_gain,
    first_bias,
    w_query,
    w_key,
    w_value,
    w_rel,
    u_bias,
    v_bias,
    w_out,
    second_gain,
    second_bias,
    w_up,
    b_up,
    w_down,
    b_down,
    w_comp,
    b_comp,
    cot_out,
    cot_comp,
):
    here, blocks = lax.axis_index("blk"), lax.axis_size("blk")
    segment, memory, comp_memory = segment[0], memory[0], comp_memory[0]
    cot_out, cot_comp = cot_out[0], cot_comp[0]
    rows, width = segment.shape
    heads = H // blocks
    cols = heads * DH
    parts = (comp_memory.shape[0], memory.shape[0], rows)
    block = sum(parts)
    count = lax.axis_size("dp").bit_length() - 1
    core, blk = ("dp", 0), ("blk", 0)
    near = [("dp", 1)]
    rest = [("dp", bit) for bit in range(2, count)]
    mate = side(*core)

    order = Order()
    weights = (first_gain, first_bias, w_query, w_key, w_value)

    windows = memory.reshape(parts[1] // RATE, RATE * width)
    far_seg = swap(segment, *blk)
    far_rest = swap(jnp.concatenate([memory, comp_memory], 0), *blk)
    cot_mate = swap(cot_out, *core)

    new_compressed = (matmul(windows, w_comp) + b_comp.astype(wide)).astype(narrow)
    grad_b_comp = jnp.sum(cot_comp.astype(wide), 0)
    grad_comp = outer(windows, cot_comp).astype(narrow)

    sinus = gate(order, sinus_table())
    relative = matmul(sinus, lax.dynamic_slice_in_dim(w_rel, here * cols, cols, 1)).astype(narrow)

    own_seg, own_mem, own_comp, q_own = project(
        order, here, (segment, memory, comp_memory), (rows, parts[1], parts[0]), True, weights, cols
    )
    far_seg, q_far = project(
        order, here, [far_seg], (rows,), True, weights, cols, after=[relative, new_compressed, grad_comp]
    )
    far_mem, far_comp = project(
        order, here, [far_rest], (parts[1], parts[0]), False, weights, cols
    )
    own, other = (own_comp, own_mem, own_seg), (far_comp, far_mem, far_seg)
    comp_share = lax.psum_scatter(gate(order, grad_comp), ("dp", "blk"), scatter_dimension=0, tiled=True)
    inputs = [q_own, q_far, u_bias, v_bias]
    for part in (1, 2):
        inputs += [[t[part] for t in own], [t[part] for t in other]]
    inputs += [relative]
    mine, received, probs = [], [], []
    per = heads // 2
    for first in range(0, heads, per):
        own_heads, far_heads, kept = attend(order, here, mem_start[0], parts, inputs, first, per)
        mine.append(own_heads)
        received.append(swap(far_heads, *blk))
        probs.append(kept)

    (
        layer_out,
        packed,
        attended_keep,
        gelu_theirs,
        gelu_mine,
        d_pre_theirs,
        d_pre_mine,
        d_hidden,
        da_mine,
        da_theirs,
        grad_b_up,
        grad_second_gain,
        grad_second_bias,
        grad_b_down,
    ) = middle(
        order, here, mate, mine, received, segment, cot_out, w_out, second_gain, second_bias, w_up, b_up, w_down, b_down
    )

    gelu_mate = swap(gelu_theirs, *core)
    da_far = swap(da_theirs, *blk)
    d_pre_mate = swap(d_pre_theirs, *core)
    packed_mate = swap(packed, *core)
    units = gelu_mine.shape[1]
    jobs = (
        ("grad_down", near + [blk] + rest, (gelu_mine, 0, units), (gelu_mate, 0, units), (cot_out, 0, width), (cot_mate, 0, width)),
        ("grad_up", [blk] + rest[:1] + near + rest[1:], (packed, 0, width), (packed_mate, 0, width), (d_pre_mine, 0, units), (d_pre_mate, 0, units)),
        ("grad_out", rest[:1] + near + rest[1:] + [blk], (attended_keep, 0, cols), (packed_mate, 2 * width, cols), (packed, width, width), (packed_mate, width, width)),
    )
    send, keep = [], []
    for job in jobs:
        after = [da_far] if job is jobs[1] else []
        send += outer_pairs(order, [job[2:]], [1 - side(*job[1][0])], job[0], after)
    keep = outer_pairs(order, [job[2:] for job in jobs], [side(*job[1][0]) for job in jobs], "grad_keep")
    middle_steps = [job[1] for job in jobs]
    middle_sum = Scatter(order, "sum_middle", list(zip(send, keep, middle_steps)))

    back = []
    for number in range(2):
        back.append(attend_back(order, here, parts, probs[number], inputs, da_mine, da_far, number * per, per))
        middle_sum.step(4 if number == 0 else 2)
        if number == 0:
            comp_gathered = lax.all_gather(gate(order, comp_share), ("dp", "blk"), axis=0, tiled=True)
    dq_own, dq_far, d_key, d_value, d_relative, grad_u, grad_v = zip(*back)
    normed = [t[0] for t in own + other]
    chunk, extra = 4 * width // lax.axis_size("dp"), 16
    grads, by_gain, by_bias = grad_heads(
        order, here, parts, normed, sinus, dq_own, dq_far, d_key, d_value, d_relative, w_query, w_key, w_value, chunk, extra
    )
    middle_sum.step()
    grads, by_gain, by_bias = gate(order, grads, by_gain, by_bias)

    grad_first_bias = by_bias.reshape(width)
    grad_first_gain = (by_gain.reshape(width) - first_bias.astype(wide) * grad_first_bias) / first_gain.astype(wide)

    def spread(vectors):
        return lax.dynamic_update_slice_in_dim(
            jnp.zeros((width,), wide), jnp.concatenate(vectors, 1).reshape(cols), here * cols, 0
        )

    vectors = [
        grad_first_gain,
        grad_first_bias,
        spread(grad_u),
        spread(grad_v),
        grad_second_gain.reshape(-1),
        grad_second_bias.reshape(-1),
        grad_b_up.reshape(-1),
        grad_b_down.reshape(-1),
        grad_b_comp,
    ]

    shares = lax.axis_size("dp")
    beside = jnp.concatenate(vectors).reshape(-1, cols)
    upper = beside.astype(narrow)
    beside = jnp.concatenate([upper, (beside - upper.astype(wide)).astype(narrow)], 0)
    per = -(-beside.shape[0] // shares)
    beside = jnp.pad(beside, ((0, per * shares - beside.shape[0]), (0, 0))).reshape(shares, per, cols)
    grads = lax.dynamic_update_slice(grads.reshape(shares, chunk + extra, cols), beside, (0, chunk, 0))
    heads_share = lax.psum_scatter(grads, "dp", scatter_dimension=0, tiled=True)

    d_normed_own, d_normed_far = segment_back(
        order, here, dq_own, dq_far, d_key, d_value, w_query, w_key, w_value, block
    )
    middle_sum.step()
    middle_gather = Gather(
        order, "join_middle", [(share, steps[1:]) for share, steps in zip(middle_sum.keep, middle_steps)]
    )
    middle_gather.step()
    d_normed_received = swap(gate(order, d_normed_far), *blk)
    full_comp = widen(order, comp_gathered, "full_comp")
    d_segment = finish(order, segment, d_hidden, d_normed_own, d_normed_received, first_gain)
    middle_gather.step()
    heads_gathered = lax.all_gather(gate(order, heads_share), ("dp", "blk"), axis=0, tiled=True)
    middle_gather.step()
    sums = heads_gathered[:, chunk : chunk + per].astype(wide).reshape(shares, blocks, per, cols)
    sums = jnp.sum(sums, 1).reshape(shares * per, cols)
    small = sum(vector.shape[0] for vector in vectors) // cols
    sums = (sums[:small] + sums[small : 2 * small]).reshape(-1)
    split = []
    at = 0
    for vector in vectors:
        split.append(sums[at : at + vector.shape[0]])
        at += vector.shape[0]

    devices = 2 << count
    up_rows = width * 2 // devices
    down_value, up_value, out_value = middle_gather.values
    down_beside, up_beside, out_beside = (
        swap(value, *steps[0]) for value, steps in zip(middle_gather.values, middle_steps)
    )

    def by_rows(pieces, whose, steps, total_rows, name, before=None):
        blocks = devices // 4
        chunk = total_rows // devices
        return assemble(
            order,
            pieces,
            whose,
            blocks,
            [place_of([core, steps[0]]), place_of(steps[1:])],
            (total_rows, width),
            (total_rows // 4, width // 2),
            lambda outer_place, part: (outer_place, part),
            lambda inner_place: (inner_place * chunk, 0),
            2,
            name,
            before,
        )

    def up_out(pieces, whose, before=None):
        return assemble(
            order,
            pieces,
            whose,
            devices // 4,
            [place_of([core, middle_steps[1][0]]), place_of(middle_steps[1][1:])],
            (width, FF),
            (width // 2, FF // 4),
            lambda outer_place, part: (outer_place % 2, outer_place // 2 * 2 + part),
            lambda inner_place: (inner_place * up_rows, 0),
            2,
            "full_up",
            before,
        )

    full_down = by_rows([down_value, swap(down_value, *core)], (0, 2), middle_steps[0], FF, "full_down")
    full_up = up_out([up_value, swap(up_value, *core)], (0, 2))
    out_beside = gate(order, out_beside)
    out_pieces = [out_value, out_beside, swap(out_value, *core), swap(out_beside, *core)]
    full_out = by_rows(out_pieces, (0, 1, 2, 3), middle_steps[2], width, "full_out")
    down_beside, up_beside = gate(order, down_beside, up_beside)
    down_far, up_far = swap(down_beside, *core), swap(up_beside, *core)
    full_query, full_key, full_value, full_rel = widen_heads(
        order, heads_gathered.reshape(-1, cols), chunk, extra, width, cols, "full_heads", [sums]
    )
    full_down = by_rows([down_beside, down_far], (1, 3), middle_steps[0], FF, "full_down", full_down)
    full_up = up_out([up_beside, up_far], (1, 3), full_up)
    return (
        layer_out[None],
        d_segment[None],
        new_compressed[None],
        split[0],
        split[1],
        full_query,
        full_key,
        full_value,
        full_rel,
        split[2],
        split[3],
        full_out,
        split[4],
        split[5],
        full_up,
        split[6],
        full_down,
        split[7],
        full_comp,
        split[8],
    )


def solution(mesh):
    rows = P("dp", "blk", None)
    in_specs = (rows,) * 3 + (P("dp"),) + (P(),) * 17 + (rows,) * 2
    out_specs = (rows,) * 3 + (P(),) * 17
    return jax.shard_map(
        on_device, mesh=mesh, in_specs=in_specs, out_specs=out_specs, check_vma=False
    )
```

```python
from functools import partial

import jax
import jax.numpy as jnp
from jax import lax
from jax.experimental import pallas as pl
from jax.experimental.pallas import tpu as pltpu
from jax.sharding import PartitionSpec as P

D = 1024
H = 8
DH = 128
FF = 4096
CMEM = 512
RATE = 3
KEYS = 2432

TILE = 192
FF_TILE = 512
epsilon = 1e-05
negative = -1e30
wide = jnp.float32
narrow = jnp.bfloat16
MIB = 1 << 20


def dot(left, right, left_dim, right_dim):
    return lax.dot_general(
        left, right, (((left_dim,), (right_dim,)), ((), ())), preferred_element_type=wide
    )


def shape(rows, cols, dtype=narrow):
    return jax.ShapeDtypeStruct((rows, cols), dtype)


def whole(rows, cols):
    return pl.BlockSpec((rows, cols), lambda *_: (0, 0))


def numbers(values):
    return jnp.stack([jnp.asarray(value, jnp.int32) for value in values])


class Order:
    def __init__(self):
        self.last = []

    def call(self, kernel, name, scalars, arrays, grid, in_specs, out_specs, out_shape, scratch=(), after=(), aliases=()):
        count = len(arrays)
        after = list(after) + self.last

        def body(scalar_ref, *refs):
            kernel(scalar_ref, *refs[:count], *refs[count + len(after) :])

        out = pl.pallas_call(
            body,
            grid_spec=pltpu.PrefetchScalarGridSpec(
                num_scalar_prefetch=1,
                grid=grid,
                in_specs=list(in_specs) + [pl.BlockSpec(memory_space=pl.ANY)] * len(after),
                out_specs=out_specs,
                scratch_shapes=list(scratch),
            ),
            out_shape=out_shape,
            input_output_aliases={1 + i: o for i, o in aliases},
            compiler_params=pltpu.CompilerParams(vmem_limit_bytes=60 * MIB),
            cost_estimate=pl.CostEstimate(
                flops=1000, bytes_accessed=1000, transcendentals=0
            ),
            name=name,
        )(scalars if hasattr(scalars, "ndim") else numbers(scalars), *arrays, *after)
        self.last = [out[-1] if isinstance(out, (list, tuple)) else out]
        return out


def swap(value, axis, bit=0):
    pairs = [(source, source ^ (1 << bit)) for source in range(lax.axis_size(axis))]
    return lax.ppermute(value, axis, pairs)


def side(axis, bit=0):
    return (lax.axis_index(axis) >> bit) & 1


def place_of(steps):
    place = jnp.int32(0)
    for axis, bit in steps:
        place = place * 2 + side(axis, bit)
    return place


def add_split(order, chains, steps, name):
    in_specs, out_specs, out_shape, arrays = [], [], [], []
    for number, (kept, received, _) in enumerate(chains):
        rows, cols = kept.shape
        block = rows // 2 // steps
        theirs = pl.BlockSpec((block, cols), lambda i, ids, n=number: ((1 - ids[n]) * steps + i, 0))
        ours = pl.BlockSpec((block, cols), lambda i, ids, n=number: (ids[n] * steps + i, 0))
        arrays += [kept, received, kept, received]
        in_specs += [theirs, theirs, ours, ours]
        out_specs += [pl.BlockSpec((block, cols), lambda i, ids: (i, 0))] * 2
        out_shape += [shape(rows // 2, cols)] * 2

    def kernel(ids, *refs):
        ins, outs = refs[: 4 * len(chains)], refs[4 * len(chains) :]
        for number, out in enumerate(outs):
            a, b = ins[2 * number], ins[2 * number + 1]
            out[...] = (a[...].astype(wide) + b[...].astype(wide)).astype(narrow)

    out = order.call(kernel, name, [c[2] for c in chains], arrays, (steps,), in_specs, out_specs, out_shape)
    return [(out[2 * n], out[2 * n + 1]) for n in range(len(chains))]


def add(order, pairs, name):
    arrays = [value for pair in pairs for value in pair]

    def kernel(ids, *refs):
        for number, out in enumerate(refs[len(arrays) :]):
            a, b = refs[2 * number], refs[2 * number + 1]
            out[...] = (a[...].astype(wide) + b[...].astype(wide)).astype(narrow)

    return order.call(
        kernel,
        name,
        order.zero,
        arrays,
        (1,),
        [whole(*a.shape) for a in arrays],
        [whole(*a.shape) for a, _ in pairs],
        [shape(*a.shape) for a, _ in pairs],
    )


def gate(order, *values):
    place = pl.BlockSpec(memory_space=pl.ANY)
    out = order.call(
        lambda ids, *refs: None,
        "gate",
        order.zero,
        values,
        (1,),
        [place] * len(values),
        [place] * len(values),
        [jax.ShapeDtypeStruct(value.shape, value.dtype) for value in values],
        aliases=[(n, n) for n in range(len(values))],
    )
    return out[0] if len(values) == 1 else out


class Scatter:
    def __init__(self, order, name, chains):
        self.order, self.name = order, name
        self.steps = [steps for _, _, steps in chains]
        self.keep = [keep for _, keep, _ in chains]
        self.received = [swap(send, *steps[0]) for send, _, steps in chains]
        self.at = 0

    def step(self, blocks=1):
        self.at += 1
        if self.at == len(self.steps[0]):
            self.keep = add(self.order, list(zip(self.keep, self.received)), self.name)
            return self.keep
        chains = [
            (keep, received, side(*steps[self.at]))
            for keep, received, steps in zip(self.keep, self.received, self.steps)
        ]
        halves = add_split(self.order, chains, blocks, self.name)
        self.keep = [keep for _, keep in halves]
        self.received = [swap(send, *steps[self.at]) for (send, _), steps in zip(halves, self.steps)]


def join(order, pairs, name):
    arrays = [value for pair in pairs for value in pair]

    def kernel(ids, *refs):
        for number, out in enumerate(refs[len(arrays) :]):
            a, b = refs[2 * number], refs[2 * number + 1]
            rows = a.shape[0]
            out[0:rows, :] = a[...]
            out[rows:, :] = b[...]

    outs = [(2 * a.shape[0], a.shape[1]) for a, _ in pairs]
    return order.call(
        kernel,
        name,
        order.zero,
        arrays,
        (1,),
        [whole(*a.shape) for a in arrays],
        [whole(*out) for out in outs],
        [shape(*out) for out in outs],
    )


class Gather:
    def __init__(self, order, name, chains):
        self.order, self.name = order, name
        self.values = [value for value, _ in chains]
        self.steps = [list(steps) for _, steps in chains]
        self.send()

    def send(self):
        self.received = [swap(value, *steps.pop()) for value, steps in zip(self.values, self.steps)]

    def step(self):
        self.values = join(self.order, list(zip(self.values, self.received)), self.name)
        if self.steps[0]:
            self.send()


def assemble(order, pieces, whose, blocks, places, out_shape, out_block, index, inside, splits, name, before=None):
    rows, cols = pieces[0].shape
    chunk, part = rows // blocks, cols // splits
    count = len(pieces)

    def kernel(ids, *refs):
        out = refs[-1]
        number = pl.program_id(0)

        def copy(ref):
            for r in range(blocks):
                row, col = inside(r ^ ids[1])
                out[pl.ds(pl.multiple_of(row, 8), chunk), pl.ds(pl.multiple_of(col, 128), part)] = ref[
                    r * chunk : (r + 1) * chunk, :
                ].astype(wide)

        for n, ref in enumerate(refs[:count]):
            pl.when(number == n)(partial(copy, ref))

    def piece_spec(n):
        return pl.BlockSpec(
            (rows, part), lambda i, j, ids: (0, jnp.where(i == n, j, jnp.where(i < n, 0, splits - 1)))
        )

    def out_index(i, j, ids):
        outer_place = whose[0]
        for n, place in enumerate(whose[1:]):
            outer_place = jnp.where(i == n + 1, place, outer_place)
        return index(outer_place ^ ids[0], j)

    more = [] if before is None else [before]
    return order.call(
        kernel,
        name,
        places,
        list(pieces) + more,
        (count, splits),
        [piece_spec(n) for n in range(count)] + [pl.BlockSpec(memory_space=pl.ANY)] * len(more),
        pl.BlockSpec(out_block, out_index),
        shape(*out_shape, wide),
        aliases=[(count, 0)] if more else [],
    )


def widen(order, value, name):
    rows, cols = value.shape
    steps = 4

    def kernel(ids, ref, out):
        out[...] = ref[...].astype(wide)

    at = pl.BlockSpec((rows // steps, cols), lambda i, ids: (i, 0))
    return order.call(kernel, name, [0], [value], (steps,), [at], at, shape(rows, cols, wide))


def take_apart(order, values, lengths):
    width = values.shape[1]

    def kernel(ids, ref, *outs):
        row = 0
        for out, length in zip(outs, lengths):
            for at in range(0, length, width):
                out[at : at + width] = ref[row, :]
                row += 1

    return order.call(
        kernel,
        "take_apart",
        order.zero,
        [values],
        (1,),
        [whole(*values.shape)],
        [pl.BlockSpec((length,), lambda *_: (0,)) for length in lengths],
        [jax.ShapeDtypeStruct((length,), wide) for length in lengths],
    )


def widen_heads(order, gathered, chunk, extra, width, cols, name, after):
    arrays = 4
    rows = gathered.shape[0] // arrays
    count = rows // (chunk + extra)

    def kernel(ids, ref, *outs):
        def copy(out):
            for r in range(count):
                at = r * (chunk + extra)
                row, col = r // 2 * chunk, r % 2 * cols
                out[row : row + chunk, col : col + cols] = ref[at : at + chunk, :].astype(wide)

        for number, out in enumerate(outs):
            pl.when(pl.program_id(0) == number)(partial(copy, out))

    return order.call(
        kernel,
        name,
        order.zero,
        [gathered],
        (arrays,),
        [pl.BlockSpec((rows, cols), lambda i, ids: (i, 0))],
        [whole(width, width)] * arrays,
        [shape(width, width, wide)] * arrays,
        after=after,
    )


def project_kernel(count, lengths, ids, *refs):
    parts, (gain, bias, wq, wk, wv), outs = refs[:count], refs[count : count + 5], refs[count + 5 :]
    if count < len(lengths):
        firsts = [sum(lengths[:n]) for n in range(len(lengths))]
        parts = [parts[0].at[first : first + length, :] for first, length in zip(firsts, lengths)]
        count = len(lengths)
    for number, part in enumerate(parts):
        normed, k, v = outs[3 * number : 3 * number + 3]
        values = part[...].astype(wide)
        centred = values - jnp.mean(values, -1, keepdims=True)
        inverse = lax.rsqrt(jnp.mean(centred * centred, -1, keepdims=True) + epsilon)
        low = (centred * inverse * gain[...].astype(wide) + bias[...].astype(wide)).astype(narrow)
        normed[...] = low
        k[...] = dot(low, wk[...], 1, 0).astype(narrow)
        v[...] = dot(low, wv[...], 1, 0).astype(narrow)
        if number == 0 and len(outs) > 3 * count:
            outs[-1][...] = dot(low, wq[...], 1, 0)


def project(order, here, parts, lengths, query, weights, cols, after=()):
    gain, bias, wq, wk, wv = weights
    width = wq.shape[0]
    weight = pl.BlockSpec((width, cols), lambda i, ids: (0, ids[0]))
    unused = whole(16, 128)
    out_shape = [s for n in lengths for s in (shape(n, width), shape(n, cols), shape(n, cols))]
    if query:
        out_shape.append(shape(lengths[0], cols, wide))
    out = order.call(
        partial(project_kernel, len(parts), lengths),
        "project",
        order.here,
        list(parts) + [gain[None], bias[None], wq, wk, wv],
        (1,),
        [whole(*p.shape) for p in parts] + [whole(1, width)] * 2 + [weight if query else unused, weight, weight],
        [whole(*o.shape) for o in out_shape],
        out_shape,
        after=after,
    )
    triples = [tuple(out[3 * n : 3 * n + 3]) for n in range(len(lengths))]
    return triples + ([out[-1]] if query else [])


def tiles_of(seg, keys, tile):
    tiles = []
    for first in range(0, seg, tile):
        used = keys - seg + first + tile
        cols = -(-used // 128) * 128
        tiles.append((first, cols, keys - cols, cols - used))
    return tiles


def turned(values):
    order = 7 - lax.broadcasted_iota(jnp.int32, (8, values.shape[1]), 0)
    parts = [jnp.take_along_axis(values[at : at + 8], order, 0) for at in range(0, values.shape[0], 8)]
    return jnp.concatenate(parts, 0)


def unskew(grid, tile, cols, pad):
    parts = []
    order = 7 - lax.broadcasted_iota(jnp.int32, (8, cols), 0)
    for at in range(0, tile, 8):
        rows = jnp.take_along_axis(grid[at : at + 8], order, 0)
        parts.append(pltpu.roll(rows, tile - 1 + pad - at - 7, 1, stride=1, stride_axis=0))
    return jnp.concatenate(parts, 0)


def spans(parts, here):
    out = []
    at = 0
    for length in parts:
        own = pl.multiple_of(2 * at + here * length, 16)
        far = pl.multiple_of(2 * at + (1 - here) * length, 16)
        out.append((pl.ds(at, length), pl.ds(own, length), pl.ds(far, length)))
        at += length
    return out


def place_parts(parts, here, own, far, out):
    for (_, own_rows, far_rows), own_part, far_part in zip(spans(parts, here), own, far):
        out[own_rows, :] = own_part[...]
        out[far_rows, :] = far_part[...]


def place_queries(parts, here, q_own, q_far, u, v, qc, qp):
    ((_, own_rows, far_rows),) = spans(parts[2:], here)
    for ref, rows in ((q_own, own_rows), (q_far, far_rows)):
        qc[rows, :] = (ref[...] + u[...].astype(wide)).astype(narrow)
        qp[rows, :] = (ref[...] + v[...].astype(wide)).astype(narrow)


def attend_kernel(parts, ids, q_own, q_far, u, v, *refs):
    k_own, k_far, v_own, v_far = refs[0:3], refs[3:6], refs[6:9], refs[9:12]
    rel, out_own, out_far, probs_ref, qc, qp, ks, vs, outs = refs[12:]
    here, start = ids[0], ids[1]
    place_queries(parts, here, q_own, q_far, u, v, qc, qp)
    place_parts(parts, here, k_own, k_far, ks)
    place_parts(parts, here, v_own, v_far, vs)
    seg, keys = qc.shape[0], ks.shape[0]
    past = keys - seg
    factor = DH**-0.5 * 1.4426950408889634
    for first, cols, base, pad in tiles_of(seg, keys, TILE):
        rows = pl.ds(first, TILE)
        content = dot(qc[rows, :], ks[0:cols, :], 1, 1)
        table = dot(qp[rows, :], rel[base : base + cols, :], 1, 1)
        table = pltpu.roll(table, cols - (TILE - 1 + pad), 1, stride=1, stride_axis=0)
        scores = content + table
        left = scores[:, :CMEM]
        lane = lax.broadcasted_iota(jnp.int32, left.shape, 1)
        left = jnp.where(lane >= start, left, negative)
        edge = (past + first) // 128 * 128
        right = scores[:, edge:]
        lane = lax.broadcasted_iota(jnp.int32, right.shape, 1) + (edge - past - first)
        row = lax.broadcasted_iota(jnp.int32, right.shape, 0)
        right = jnp.where(lane <= row, right, negative)
        scores = jnp.concatenate([left, scores[:, CMEM:edge], right], 1)
        largest = jnp.max(scores, -1, keepdims=True)
        probs = jnp.exp2(scores * factor - largest * factor)
        probs = (probs * (1.0 / jnp.sum(probs, -1, keepdims=True))).astype(narrow)
        probs_ref[0, rows, 0:cols] = probs
        outs[rows, :] = dot(probs, vs[0:cols, :], 1, 0).astype(narrow)
    ((_, own_rows, far_rows),) = spans(parts[2:], here)
    out_own[...] = outs[own_rows, :]
    out_far[...] = outs[far_rows, :]


def part_specs(parts, first):
    return [pl.BlockSpec((length, DH), lambda h, ids: (0, h + first)) for length in parts]


def attend(order, here, start, parts, inputs, first, heads):
    q_own, q_far, u, v, k_own, k_far, v_own, v_far, rel = inputs
    rows, keys = parts[2], rel.shape[0]
    query = pl.BlockSpec((rows, DH), lambda h, ids: (0, h + first))
    bias = pl.BlockSpec((1, DH), lambda h, ids: (0, h + first + ids[0] * (H // 2)))
    out = pl.BlockSpec((rows, DH), lambda h, ids: (0, h))
    seg = 2 * rows
    return order.call(
        partial(attend_kernel, parts),
        "attend",
        order.attend,
        [q_own, q_far, u, v, *k_own, *k_far, *v_own, *v_far, rel],
        (heads,),
        [query, query, bias, bias]
        + part_specs(parts, first) * 4
        + [pl.BlockSpec((keys, DH), lambda h, ids: (0, h + first))],
        [out, out, pl.BlockSpec((1, seg, keys), lambda h, ids: (h, 0, 0))],
        [shape(rows, heads * DH)] * 2 + [jax.ShapeDtypeStruct((heads, seg, keys), narrow)],
        [pltpu.VMEM((seg, DH), narrow)] * 2
        + [pltpu.VMEM((keys, DH), narrow)] * 2
        + [pltpu.VMEM((seg, DH), narrow)],
    )


def attend_back_kernel(parts, ids, probs_ref, q_own, q_far, u, v, *refs):
    k_own, k_far, v_own, v_far = refs[0:3], refs[3:6], refs[6:9], refs[9:12]
    rel, da_own, da_far, dq_own, dq_far, dk_ref, dv_ref, drel_ref, gu_ref, gv_ref = refs[12:22]
    qc_ref, qp_ref, ks, vs, das, dqs, stage, key_sum, value_sum, rel_sum = refs[22:]
    here = ids[0]
    place_queries(parts, here, q_own, q_far, u, v, qc_ref, qp_ref)
    place_parts(parts, here, k_own, k_far, ks)
    place_parts(parts, here, v_own, v_far, vs)
    ((_, own_rows, far_rows),) = spans(parts[2:], here)
    das[own_rows, :] = da_own[...]
    das[far_rows, :] = da_far[...]
    seg, keys = qc_ref.shape[0], ks.shape[0]
    scale = DH**-0.5

    grad_u = jnp.zeros((1, DH), wide)
    grad_v = jnp.zeros((1, DH), wide)
    for step, (first, cols, base, pad) in enumerate(tiles_of(seg, keys, TILE)[::-1]):
        rows = pl.ds(first, TILE)
        probs = probs_ref[0, rows, 0:cols]
        probs_wide = probs.astype(wide)
        d_out, qc, qp = das[rows, :], qc_ref[rows, :], qp_ref[rows, :]
        d_probs = dot(d_out, vs[0:cols, :], 1, 1)
        weighted = probs_wide * d_probs
        d_scores = weighted - probs_wide * jnp.sum(weighted, -1, keepdims=True)
        d_low = d_scores.astype(narrow)
        d_table = unskew(d_scores, TILE, cols, pad).astype(narrow)
        d_content = dot(d_low, ks[0:cols, :], 1, 0)
        d_position = turned(dot(d_table, rel[base : base + cols, :], 1, 0))
        grad_u += jnp.sum(d_content, 0, keepdims=True)
        grad_v += jnp.sum(d_position, 0, keepdims=True)
        dqs[rows, :] = ((d_content + d_position) * scale).astype(narrow)
        d_key = dot(qc, d_low, 0, 0)
        d_value = dot(d_out, probs, 0, 0)
        d_rel = dot(turned(qp.astype(wide)).astype(narrow), d_table, 0, 0)
        if step == 0:
            key_sum[...] = d_key
            value_sum[...] = d_value
            rel_sum[...] = d_rel
        else:
            key_sum[:, 0:cols] += d_key
            value_sum[:, 0:cols] += d_value
            rel_sum[:, base : base + cols] += d_rel
    gu_ref[...] = grad_u * scale
    gv_ref[...] = grad_v * scale
    drel_ref[...] = (rel_sum[...] * scale).T.astype(narrow)
    dq_own[...] = dqs[own_rows, :]
    dq_far[...] = dqs[far_rows, :]
    block = sum(parts)
    for total, factor, out in ((key_sum, scale, dk_ref), (value_sum, 1.0, dv_ref)):
        stage[...] = (total[...] * factor).T.astype(narrow)
        for rows, mine, theirs in spans(parts, here):
            out[rows, :] = stage[mine, :]
            out[pl.ds(block + rows.start, rows.size), :] = stage[theirs, :]


def attend_back(order, here, parts, probs, inputs, da_own, da_far, first, heads):
    q_own, q_far, u, v, k_own, k_far, v_own, v_far, rel = inputs
    rows, keys = parts[2], rel.shape[0]
    seg = 2 * rows
    query = pl.BlockSpec((rows, DH), lambda h, ids: (0, h + first))
    bias = pl.BlockSpec((1, DH), lambda h, ids: (0, h + first + ids[0] * (H // 2)))
    key = pl.BlockSpec((keys, DH), lambda h, ids: (0, h + first))
    query_out = pl.BlockSpec((rows, DH), lambda h, ids: (0, h))
    key_out = pl.BlockSpec((keys, DH), lambda h, ids: (0, h))
    per_head = pl.BlockSpec((1, DH), lambda h, ids: (0, h))
    small, large = pltpu.VMEM((seg, DH), narrow), pltpu.VMEM((keys, DH), narrow)
    return order.call(
        partial(attend_back_kernel, parts),
        "attend_back",
        order.here,
        [probs, q_own, q_far, u, v, *k_own, *k_far, *v_own, *v_far, rel, da_own, da_far],
        (heads,),
        [pl.BlockSpec((1, seg, keys), lambda h, ids: (h, 0, 0)), query, query, bias, bias]
        + part_specs(parts, first) * 4
        + [key, query, query],
        [query_out, query_out, key_out, key_out, key_out, per_head, per_head],
        [shape(rows, heads * DH)] * 2
        + [shape(keys, heads * DH)] * 3
        + [shape(1, heads * DH, wide)] * 2,
        [small, small, large, large, small, small, large] + [pltpu.VMEM((DH, keys), wide)] * 3,
    )


def middle_kernel(own_pieces, far_pieces, ids, *refs):
    mine, refs = refs[:own_pieces], refs[own_pieces:]
    received, refs = refs[:far_pieces], refs[far_pieces:]
    segment, cot, w_out, gain, bias, w_up, b_up, w_down, b_down = refs[:9]
    (layer_out, packed, att_keep, gelu_theirs, gelu_mine, d_theirs, d_mine, d_hidden, da_mine, da_theirs, g_up, g_gain, g_bias, g_down,
     normal, inverse, layer, back) = refs[9:]
    normed, d_branch, att_send = packed.at[:, 0:D], packed.at[:, D : 2 * D], packed.at[:, 2 * D :]
    step = pl.program_id(0)
    steps = pl.num_programs(0)
    here = ids[0]
    half = D // 2

    @pl.when(step == 0)
    def _():
        own = jnp.concatenate([ref[...] for ref in mine], 1)
        far = jnp.concatenate([ref[...] for ref in received], 1)
        own_rows = pl.ds(pl.multiple_of(here * half, 128), half)
        far_rows = pl.ds(pl.multiple_of((1 - here) * half, 128), half)
        hidden = segment[...].astype(wide) + dot(own, w_out[own_rows, :], 1, 0) + dot(far, w_out[far_rows, :], 1, 0)
        same = here == ids[1]
        att_keep[...] = jnp.where(same, own, far)
        att_send[...] = jnp.where(same, far, own)
        centred = hidden - jnp.mean(hidden, -1, keepdims=True)
        scale = lax.rsqrt(jnp.mean(centred * centred, -1, keepdims=True) + epsilon)
        inverse[...] = scale
        normal[...] = centred * scale
        normed[...] = (normal[...] * gain[...].astype(wide) + bias[...].astype(wide)).astype(narrow)
        layer[...] = hidden + b_down[...].astype(wide)
        back[...] = jnp.zeros_like(back)

    t = dot(normed[...], w_up[...], 1, 0) + b_up[...].astype(wide)
    d_gelu = dot(cot[...], w_down[...], 1, 1)
    square = t * t
    slope = 0.7978845608028654
    bent = jnp.tanh(slope * t * (1.0 + 0.044715 * square))
    rise = 0.5 * (1.0 + bent)
    gelu = (t * rise).astype(narrow)
    change = rise + (0.5 * slope) * t * (1.0 - bent * bent) * (1.0 + (3 * 0.044715) * square)
    d_pre = (d_gelu * change).astype(narrow)
    layer[...] += dot(gelu, w_down[...], 1, 0)
    back[...] += dot(d_pre, w_up[...], 1, 1)
    g_up[...] = jnp.sum(d_pre.astype(wide), 0, keepdims=True)

    @pl.when(step < steps // 2)
    def _():
        gelu_theirs[...] = gelu
        d_theirs[...] = d_pre

    @pl.when(step >= steps // 2)
    def _():
        gelu_mine[...] = gelu
        d_mine[...] = d_pre

    @pl.when(step == steps - 1)
    def _():
        layer_out[...] = layer[...].astype(narrow)
        e, n = back[...], normal[...]
        cot_wide = cot[...].astype(wide)
        en = e * n
        g_gain[...] = jnp.sum(en, 0, keepdims=True)
        g_bias[...] = jnp.sum(e, 0, keepdims=True)
        g_down[...] = jnp.sum(cot_wide, 0, keepdims=True)
        by = gain[...].astype(wide)
        inner = e * by - jnp.mean(e * by, -1, keepdims=True) - n * jnp.mean(en * by, -1, keepdims=True)
        d_wide = cot_wide + inner * inverse[...]
        d_hidden[...] = d_wide
        low = d_wide.astype(narrow)
        d_branch[...] = low
        own_rows = pl.ds(pl.multiple_of(here * half, 128), half)
        far_rows = pl.ds(pl.multiple_of((1 - here) * half, 128), half)
        da_theirs[...] = dot(low, w_out[far_rows, :], 1, 1).astype(narrow)
        da_mine[...] = dot(low, w_out[own_rows, :], 1, 1).astype(narrow)


def middle(order, here, core, mine, received, segment, cot, w_out, gain, bias, w_up, b_up, w_down, b_down):
    rows, width = segment.shape
    units = w_up.shape[1]
    steps = units // FF_TILE
    half = steps // 2

    def tile(j, ids):
        return jnp.where(j < half, (1 - ids[1]) * half + j, ids[1] * half + j - half)

    up = pl.BlockSpec((width, FF_TILE), lambda j, ids: (0, tile(j, ids)))
    down = pl.BlockSpec((FF_TILE, width), lambda j, ids: (tile(j, ids), 0))
    unit = pl.BlockSpec((1, FF_TILE), lambda j, ids: (0, tile(j, ids)))
    theirs = pl.BlockSpec((rows, FF_TILE), lambda j, ids: (0, jnp.minimum(j, half - 1)))
    ours = pl.BlockSpec((rows, FF_TILE), lambda j, ids: (0, jnp.maximum(j - half, 0)))
    row, vector = whole(rows, width), whole(1, width)
    heads = whole(rows, width // 2)
    return order.call(
        partial(middle_kernel, len(mine), len(received)),
        "middle",
        order.both,
        list(mine) + list(received) + [segment, cot, w_out, gain, bias, w_up, b_up, w_down, b_down],
        (steps,),
        [whole(*a.shape) for a in list(mine) + list(received)]
        + [row, row, whole(width, width), vector, vector, up, unit, down, vector],
        [row, whole(rows, 5 * width // 2), heads, theirs, ours, theirs, ours, row, heads, heads, unit]
        + [vector] * 3,
        [shape(rows, width), shape(rows, 5 * width // 2), shape(rows, width // 2)]
        + [shape(rows, units // 2)] * 4
        + [shape(rows, width, wide)]
        + [shape(rows, width // 2)] * 2
        + [shape(1, units, wide)]
        + [shape(1, width, wide)] * 3,
        [pltpu.VMEM((rows, width), wide), pltpu.VMEM((rows, 1), wide)] + [pltpu.VMEM((rows, width), wide)] * 2,
    )


def outer_pairs(order, jobs, whichs, name, after=()):
    arrays, in_specs, out_specs, out_shape, spans_of = [], [], [], [], []
    step = 0
    for number, job in enumerate(jobs):
        rows, cols = job[0][2] // 2, job[2][2]
        block = min(rows, 512)
        first, steps = step, rows // block
        step += steps
        spans_of.append((first, steps))

        def at(i, first=first, steps=steps):
            return jnp.clip(i - first, 0, steps - 1)

        for array, column, _ in job[:2]:
            arrays.append(array)
            in_specs.append(
                pl.BlockSpec(
                    (array.shape[0], block),
                    lambda i, ids, n=number, c=column // block, steps=steps, at=at: (0, c + ids[n] * steps + at(i)),
                )
            )
        for array, column, _ in job[2:]:
            arrays.append(array)
            in_specs.append(pl.BlockSpec((array.shape[0], cols), lambda i, ids, c=column // cols: (0, c)))
        out_specs.append(pl.BlockSpec((block, cols), lambda i, ids, at=at: (at(i), 0)))
        out_shape.append(shape(rows, cols))

    def kernel(ids, *refs):
        number = pl.program_id(0)
        for n, (first, steps) in enumerate(spans_of):

            def run(n=n):
                lo, lf, ro, rf = refs[4 * n : 4 * n + 4]
                total = dot(lo[...], ro[...], 0, 0) + dot(lf[...], rf[...], 0, 0)
                refs[4 * len(jobs) + n][...] = total.astype(narrow)

            if len(jobs) == 1:
                run()
            else:
                pl.when((number >= first) & (number < first + steps))(run)

    return order.call(
        kernel, name, whichs, arrays, (step,), in_specs, out_specs, out_shape, after=after
    )


def segment_back_kernel(count, block, ids, *refs):
    dq_own, dq_far, dk, dv = (refs[n * count : (n + 1) * count] for n in range(4))
    wq, wk, wv, own, far = refs[4 * count :]
    rows = dq_own[0].shape[0]

    def through(dq, last):
        at = pl.ds(last - rows, rows)
        total = dot(jnp.concatenate([d[...] for d in dq], 1), wq[...], 1, 1)
        total += dot(jnp.concatenate([d[at, :] for d in dk], 1), wk[...], 1, 1)
        return total + dot(jnp.concatenate([d[at, :] for d in dv], 1), wv[...], 1, 1)

    far[...] = through(dq_far, 2 * block).astype(narrow)
    own[...] = through(dq_own, block)


def segment_back(order, here, dq_own, dq_far, dk, dv, wq, wk, wv, block):
    rows, width, cols = dq_own[0].shape[0], wq.shape[0], wq.shape[1] // 2
    weight = pl.BlockSpec((width, cols), lambda i, ids: (0, ids[0]))
    arrays = [*dq_own, *dq_far, *dk, *dv]
    return order.call(
        partial(segment_back_kernel, len(dk), block),
        "segment_back",
        order.here,
        arrays + [wq, wk, wv],
        (1,),
        [whole(*a.shape) for a in arrays] + [weight] * 3,
        [whole(rows, width)] * 2,
        [shape(rows, width, wide), shape(rows, width)],
    )


def grad_heads_kernel(parts, count, chunk, extra, ids, *refs):
    normed, refs = refs[:6], refs[6:]
    sinus, refs = refs[0], refs[1:]
    dq_own, dq_far, dk, dv, drel = (refs[n * count : (n + 1) * count] for n in range(5))
    wq, wk, wv, out, by_gain, by_bias = refs[5 * count :]
    param = pl.program_id(0)

    @pl.when(param == 0)
    def _():
        by_gain[...] = jnp.zeros_like(by_gain)
        by_bias[...] = jnp.zeros_like(by_bias)

    def store(grad):
        for n in range(grad.shape[0] // chunk):
            at = n * (chunk + extra)
            out[at : at + chunk, :] = grad[n * chunk : (n + 1) * chunk, :].astype(narrow)
            out[at + chunk : at + chunk + extra, :] = jnp.zeros((extra, grad.shape[1]), narrow)

    def sums(weight, grad, d_heads):
        weight = weight[...].astype(wide)
        column = sum(jnp.sum(d.astype(wide), 0, keepdims=True) for d in d_heads)
        by_gain[...] += jnp.sum(weight * grad, 1, keepdims=True)
        by_bias[...] += jnp.sum(weight * column, 1, keepdims=True)

    def beside(refs, rows=slice(None)):
        return jnp.concatenate([ref[rows, :] for ref in refs], 1)

    @pl.when(param == 0)
    def _():
        own, far = beside(dq_own), beside(dq_far)
        grad = (dot(own, normed[2][...], 0, 0) + dot(far, normed[5][...], 0, 0)).T
        store(grad)
        sums(wq, grad, (own, far))

    for number, weight, d_heads in ((1, wk, dk), (2, wv, dv)):

        @pl.when(param == number)
        def _(weight=weight, d_heads=d_heads):
            grad = 0.0
            at = 0
            for part in normed:
                rows = part.shape[0]
                grad += dot(beside(d_heads, slice(at, at + rows)), part[...], 0, 0)
                at += rows
            grad = grad.T
            store(grad)
            sums(weight, grad, (beside(d_heads),))

    @pl.when(param == 3)
    def _():
        store(dot(beside(drel), sinus[...], 0, 0).T)


def grad_heads(order, here, parts, normed, sinus, dq_own, dq_far, dk, dv, drel, wq, wk, wv, chunk, extra):
    width, cols = wq.shape[0], wq.shape[1] // 2
    weight = pl.BlockSpec((width, cols), lambda i, ids: (0, ids[0]))
    arrays = [*normed, sinus, *dq_own, *dq_far, *dk, *dv, *drel]
    rows = width // chunk * (chunk + extra)
    return order.call(
        partial(grad_heads_kernel, parts, len(dk), chunk, extra),
        "grad_heads",
        order.here,
        arrays + [wq, wk, wv],
        (4,),
        [whole(*a.shape) for a in arrays] + [weight] * 3,
        [pl.BlockSpec((rows, cols), lambda i, ids: (i, 0)), whole(width, 1), whole(width, 1)],
        [shape(4 * rows, cols)] + [shape(width, 1, wide)] * 2,
    )


def finish_kernel(ids, segment, d_hidden, own, received, gain, out):
    values = segment[...].astype(wide)
    centred = values - jnp.mean(values, -1, keepdims=True)
    inverse = lax.rsqrt(jnp.mean(centred * centred, -1, keepdims=True) + epsilon)
    normal = centred * inverse
    scaled = (own[...] + received[...].astype(wide)) * gain[...].astype(wide)
    inner = (
        scaled
        - jnp.mean(scaled, -1, keepdims=True)
        - normal * jnp.mean(scaled * normal, -1, keepdims=True)
    )
    out[...] = (d_hidden[...] + inner * inverse).astype(narrow)


def finish(order, *arrays):
    segment, d_hidden, own, received, gain = arrays
    arrays = [segment, d_hidden, own, received, gain[None]]
    return order.call(
        finish_kernel,
        "finish",
        order.zero,
        arrays,
        (1,),
        [whole(*a.shape) for a in arrays],
        whole(*segment.shape),
        shape(*segment.shape),
    )


def sinus_table():
    fine = 64
    frequency = 10000.0 ** (-2.0 * jnp.arange(D // 2, dtype=wide) / D)
    coarse_place = KEYS - 1 - fine * jnp.arange(KEYS // fine, dtype=wide)
    fine_place = jnp.arange(fine, dtype=wide)
    coarse = (coarse_place[:, None] * frequency[None, :])[:, None, :]
    little = (fine_place[:, None] * frequency[None, :])[None, :, :]
    sin_a, cos_a, sin_b, cos_b = lax.optimization_barrier(
        (jnp.sin(coarse), jnp.cos(coarse), jnp.sin(little), jnp.cos(little))
    )
    sine = sin_a * cos_b - cos_a * sin_b
    cosine = cos_a * cos_b + sin_a * sin_b
    return jnp.concatenate([sine, cosine], -1).astype(narrow).reshape(KEYS, D)


def matmul(left, right):
    return jnp.dot(left, right, preferred_element_type=wide)


def outer(left, right):
    return dot(left, right, 0, 0)


def on_device(
    segment,
    memory,
    comp_memory,
    mem_start,
    first_gain,
    first_bias,
    w_query,
    w_key,
    w_value,
    w_rel,
    u_bias,
    v_bias,
    w_out,
    second_gain,
    second_bias,
    w_up,
    b_up,
    w_down,
    b_down,
    w_comp,
    b_comp,
    cot_out,
    cot_comp,
):
    here, blocks = lax.axis_index("blk"), lax.axis_size("blk")
    segment, memory, comp_memory = segment[0], memory[0], comp_memory[0]
    cot_out, cot_comp = cot_out[0], cot_comp[0]
    rows, width = segment.shape
    heads = H // blocks
    cols = heads * DH
    parts = (comp_memory.shape[0], memory.shape[0], rows)
    block = sum(parts)
    count = lax.axis_size("dp").bit_length() - 1
    core, blk = ("dp", 0), ("blk", 0)
    near = [("dp", 1)]
    rest = [("dp", bit) for bit in range(2, count)]
    mate = side(*core)

    order = Order()
    order.zero = jnp.zeros((1,), jnp.int32)
    order.here, order.attend, order.both, u_row, v_row, gain_row, bias_row, up_row, down_row = gate(
        order,
        numbers([here]),
        numbers([here, mem_start[0]]),
        numbers([here, mate]),
        *(vector[None] for vector in (u_bias, v_bias, second_gain, second_bias, b_up, b_down)),
    )
    weights = (first_gain, first_bias, w_query, w_key, w_value)

    windows = memory.reshape(parts[1] // RATE, RATE * width)
    far_seg = swap(segment, *blk)
    far_rest = swap(jnp.concatenate([memory, comp_memory], 0), *blk)
    cot_mate = swap(cot_out, *core)

    new_compressed = (matmul(windows, w_comp) + b_comp.astype(wide)).astype(narrow)
    grad_b_comp = jnp.sum(cot_comp.astype(wide), 0)
    grad_comp = outer(windows, cot_comp).astype(narrow)

    sinus = gate(order, sinus_table())
    relative = matmul(sinus, lax.dynamic_slice_in_dim(w_rel, here * cols, cols, 1)).astype(narrow)

    own_seg, own_mem, own_comp, q_own = project(
        order, here, (segment, memory, comp_memory), (rows, parts[1], parts[0]), True, weights, cols
    )
    far_seg, q_far = project(
        order, here, [far_seg], (rows,), True, weights, cols, after=[relative, new_compressed, grad_comp]
    )
    far_mem, far_comp = project(
        order, here, [far_rest], (parts[1], parts[0]), False, weights, cols
    )
    own, other = (own_comp, own_mem, own_seg), (far_comp, far_mem, far_seg)
    comp_share = lax.psum_scatter(gate(order, grad_comp), ("dp", "blk"), scatter_dimension=0, tiled=True)
    inputs = [q_own, q_far, u_row, v_row]
    for part in (1, 2):
        inputs += [[t[part] for t in own], [t[part] for t in other]]
    inputs += [relative]
    mine, received, probs = [], [], []
    per = heads // 2
    for first in range(0, heads, per):
        own_heads, far_heads, kept = attend(order, here, mem_start[0], parts, inputs, first, per)
        mine.append(own_heads)
        received.append(swap(far_heads, *blk))
        probs.append(kept)

    (
        layer_out,
        packed,
        attended_keep,
        gelu_theirs,
        gelu_mine,
        d_pre_theirs,
        d_pre_mine,
        d_hidden,
        da_mine,
        da_theirs,
        grad_b_up,
        grad_second_gain,
        grad_second_bias,
        grad_b_down,
    ) = middle(
        order, here, mate, mine, received, segment, cot_out, w_out, gain_row, bias_row, w_up, up_row, w_down, down_row
    )

    gelu_mate = swap(gelu_theirs, *core)
    da_far = swap(da_theirs, *blk)
    d_pre_mate = swap(d_pre_theirs, *core)
    packed_mate = swap(packed, *core)
    units = gelu_mine.shape[1]
    jobs = (
        ("grad_down", near + [blk] + rest, (gelu_mine, 0, units), (gelu_mate, 0, units), (cot_out, 0, width), (cot_mate, 0, width)),
        ("grad_up", [blk] + rest[:1] + near + rest[1:], (packed, 0, width), (packed_mate, 0, width), (d_pre_mine, 0, units), (d_pre_mate, 0, units)),
        ("grad_out", rest[:1] + near + rest[1:] + [blk], (attended_keep, 0, cols), (packed_mate, 2 * width, cols), (packed, width, width), (packed_mate, width, width)),
    )
    send, keep = [], []
    for job in jobs:
        after = [da_far] if job is jobs[1] else []
        send += outer_pairs(order, [job[2:]], [1 - side(*job[1][0])], job[0], after)
    keep = outer_pairs(order, [job[2:] for job in jobs], [side(*job[1][0]) for job in jobs], "grad_keep")
    middle_steps = [job[1] for job in jobs]
    middle_sum = Scatter(order, "sum_middle", list(zip(send, keep, middle_steps)))

    back = []
    for number in range(2):
        back.append(attend_back(order, here, parts, probs[number], inputs, da_mine, da_far, number * per, per))
        middle_sum.step(4 if number == 0 else 2)
        if number == 0:
            comp_gathered = lax.all_gather(gate(order, comp_share), ("dp", "blk"), axis=0, tiled=True)
    dq_own, dq_far, d_key, d_value, d_relative, grad_u, grad_v = zip(*back)
    normed = [t[0] for t in own + other]
    chunk, extra = 4 * width // lax.axis_size("dp"), 16
    grads, by_gain, by_bias = grad_heads(
        order, here, parts, normed, sinus, dq_own, dq_far, d_key, d_value, d_relative, w_query, w_key, w_value, chunk, extra
    )
    middle_sum.step()
    grads, by_gain, by_bias = gate(order, grads, by_gain, by_bias)

    grad_first_bias = by_bias.reshape(width)
    grad_first_gain = (by_gain.reshape(width) - first_bias.astype(wide) * grad_first_bias) / first_gain.astype(wide)

    def spread(vectors):
        return lax.dynamic_update_slice_in_dim(
            jnp.zeros((width,), wide), jnp.concatenate(vectors, 1).reshape(cols), here * cols, 0
        )

    vectors = [
        grad_first_gain,
        grad_first_bias,
        spread(grad_u),
        spread(grad_v),
        grad_second_gain.reshape(-1),
        grad_second_bias.reshape(-1),
        grad_b_up.reshape(-1),
        grad_b_down.reshape(-1),
        grad_b_comp,
    ]

    shares = lax.axis_size("dp")
    beside = jnp.concatenate(vectors).reshape(-1, cols)
    upper = beside.astype(narrow)
    beside = jnp.concatenate([upper, (beside - upper.astype(wide)).astype(narrow)], 0)
    per = -(-beside.shape[0] // shares)
    beside = jnp.pad(beside, ((0, per * shares - beside.shape[0]), (0, 0))).reshape(shares, per, cols)
    grads = lax.dynamic_update_slice(grads.reshape(shares, chunk + extra, cols), beside, (0, chunk, 0))
    heads_share = lax.psum_scatter(grads, "dp", scatter_dimension=0, tiled=True)

    d_normed_own, d_normed_far = segment_back(
        order, here, dq_own, dq_far, d_key, d_value, w_query, w_key, w_value, block
    )
    middle_sum.step()
    middle_gather = Gather(
        order, "join_middle", [(share, steps[1:]) for share, steps in zip(middle_sum.keep, middle_steps)]
    )
    middle_gather.step()
    d_normed_received = swap(gate(order, d_normed_far), *blk)
    full_comp = widen(order, comp_gathered, "full_comp")
    d_segment = finish(order, segment, d_hidden, d_normed_own, d_normed_received, first_gain)
    middle_gather.step()
    heads_gathered = lax.all_gather(gate(order, heads_share), ("dp", "blk"), axis=0, tiled=True)
    middle_gather.step()
    sums = heads_gathered[:, chunk : chunk + per].astype(wide).reshape(shares, blocks, per, cols)
    sums = jnp.sum(sums, 1).reshape(shares * per, cols)
    small = sum(vector.shape[0] for vector in vectors) // cols
    sums = (sums[:small] + sums[small : 2 * small]).reshape(-1)

    devices = 2 << count
    up_rows = width * 2 // devices
    down_value, up_value, out_value = middle_gather.values
    down_beside, up_beside, out_beside = (
        swap(value, *steps[0]) for value, steps in zip(middle_gather.values, middle_steps)
    )

    def by_rows(pieces, whose, steps, total_rows, name, before=None):
        blocks = devices // 4
        chunk = total_rows // devices
        return assemble(
            order,
            pieces,
            whose,
            blocks,
            [place_of([core, steps[0]]), place_of(steps[1:])],
            (total_rows, width),
            (total_rows // 4, width // 2),
            lambda outer_place, part: (outer_place, part),
            lambda inner_place: (inner_place * chunk, 0),
            2,
            name,
            before,
        )

    def up_out(pieces, whose, before=None):
        return assemble(
            order,
            pieces,
            whose,
            devices // 4,
            [place_of([core, middle_steps[1][0]]), place_of(middle_steps[1][1:])],
            (width, FF),
            (width // 2, FF // 4),
            lambda outer_place, part: (outer_place % 2, outer_place // 2 * 2 + part),
            lambda inner_place: (inner_place * up_rows, 0),
            2,
            "full_up",
            before,
        )

    full_down = by_rows([down_value, swap(down_value, *core)], (0, 2), middle_steps[0], FF, "full_down")
    full_up = up_out([up_value, swap(up_value, *core)], (0, 2))
    out_beside = gate(order, out_beside)
    out_pieces = [out_value, out_beside, swap(out_value, *core), swap(out_beside, *core)]
    full_out = by_rows(out_pieces, (0, 1, 2, 3), middle_steps[2], width, "full_out")
    down_beside, up_beside = gate(order, down_beside, up_beside)
    down_far, up_far = swap(down_beside, *core), swap(up_beside, *core)
    split = take_apart(order, sums.reshape(-1, width), [vector.shape[0] for vector in vectors])
    full_query, full_key, full_value, full_rel = widen_heads(
        order, heads_gathered.reshape(-1, cols), chunk, extra, width, cols, "full_heads", [sums]
    )
    full_down = by_rows([down_beside, down_far], (1, 3), middle_steps[0], FF, "full_down", full_down)
    full_up = up_out([up_beside, up_far], (1, 3), full_up)
    return (
        layer_out[None],
        d_segment[None],
        new_compressed[None],
        split[0],
        split[1],
        full_query,
        full_key,
        full_value,
        full_rel,
        split[2],
        split[3],
        full_out,
        split[4],
        split[5],
        full_up,
        split[6],
        full_down,
        split[7],
        full_comp,
        split[8],
    )


def solution(mesh):
    rows = P("dp", "blk", None)
    in_specs = (rows,) * 3 + (P("dp"),) + (P(),) * 17 + (rows,) * 2
    out_specs = (rows,) * 3 + (P(),) * 17
    return jax.shard_map(
        on_device, mesh=mesh, in_specs=in_specs, out_specs=out_specs, check_vma=False
    )
```
